32 devices in a mesh: group: 2 (over y), pool: 4 (over z), tensor: 4 (over x, core).
Axes of the slice: x: 2, y: 2, z: 4, core: 2. Of those that a mesh axis runs over, the one named last changes fastest.
Arguments:
- owner_map: int32 [96], P('group'), parts along dimension 0, may hold values from 0 to 3, as said below
- prompt_len: int32 [96], P(('group', 'pool')), parts along dimension 0, may hold values from 1 to 16, as said below
- memory: bfloat16 [96, 4, 256, 512], P(('group', 'pool'), 'tensor'), parts along dimension 0, may hold values from -6 to 6
- normalizer: float32 [96, 4, 256], P(('group', 'pool'), 'tensor'), parts along dimension 0, may hold values from 1 to 3
- stabilizer: float32 [96, 4], P(('group', 'pool'), 'tensor'), parts along dimension 0, may hold values from 0 to 103
- block_q: bfloat16 [96, 16, 1024], P(('group', 'pool'), None, 'tensor'), parts along dimension 0, may hold values from -1 to 2
- block_k: bfloat16 [96, 16, 1024], P(('group', 'pool'), None, 'tensor'), parts along dimension 0, may hold values from -1 to 2
- block_v: bfloat16 [96, 16, 2048], P(('group', 'pool'), None, 'tensor'), parts along dimension 0, may hold values from -6 to 6
- block_igate: bfloat16 [96, 4, 16], P(('group', 'pool'), 'tensor'), parts along dimension 0, may hold values from -8 to 103
- block_fgate: bfloat16 [96, 4, 16], P(('group', 'pool'), 'tensor'), parts along dimension 0, may hold values from -1 to 9
- step_q: bfloat16 [144, 4, 1024], P(('group', 'pool'), None, 'tensor'), parts along dimension 0, may hold values from -1 to 2
- step_k: bfloat16 [144, 4, 1024], P(('group', 'pool'), None, 'tensor'), parts along dimension 0, may hold values from -1 to 2
- step_v: bfloat16 [144, 4, 2048], P(('group', 'pool'), None, 'tensor'), parts along dimension 0, may hold values from -6 to 6
- step_igate: bfloat16 [144, 4, 4], P(('group', 'pool'), 'tensor'), parts along dimension 0, may hold values from -4 to 107
- step_fgate: bfloat16 [144, 4, 4], P(('group', 'pool'), 'tensor'), parts along dimension 0, may hold values from -1 to 9
- out_weight: bfloat16 [2048, 4096], P('tensor'), may hold values from -0.125 to 0.125
Outputs:
- block_out: bfloat16 [96, 16, 4096], P(('group', 'pool'), None, 'tensor'), parts along dimension 0
- step_out: bfloat16 [144, 4, 4096], P(('group', 'pool'), None, 'tensor'), parts along dimension 0
- memory_out: bfloat16 [144, 4, 256, 512], P(('group', 'pool'), 'tensor'), parts along dimension 0
- normalizer_out: float32 [144, 4, 256], P(('group', 'pool'), 'tensor'), parts along dimension 0
- max_out: float32 [144, 4], P(('group', 'pool'), 'tensor'), parts along dimension 0
The draws below stay inside these ranges and needn't reach their ends.
There are 2 independent parts, one for each index of `group`. The reference program is written for one: setup_inputs(seed, part) draws one part's arguments, and reference() takes and returns one part's arrays. A program takes and returns all parts, laid end to end along the dimension named above; an argument that names none is the same for every part. Nothing has to cross between parts.
Inputs may be any that keep to these rules, and one draw needn't show every extreme that they name: `owner_map`: some owner receives exactly 18 requests and none more; the requests of one pool index (rows r * 12 to r * 12 + 11) name one owner at most 5 times, and some exactly 5 times. `prompt_len`: some request has exactly 16.
All inputs are finite; a program needn't handle non-finite values.
Results may differ from the reference program's by a relative error of at most 0.009.
Values may be sent and summed in bfloat16 or wider, within the bound.
A program may use at most 128 MiB of HBM per device.

```python
import math
import jax
import jax.numpy as jnp
from jax import lax

D = 4096
HEADS = 4
DQK = 256
DV = 512
BLOCK = 16
STEPS = 4
R_DEV = 12
R = 48
CAP = 18
SLOTS = 72
N_POOL = 4
N_TENSOR = 4


def route_table(key):
    key = jax.random.fold_in(key, 101)
    pool_count = R // R_DEV
    order_key, spread_key = jax.random.split(key)
    owner_order = jax.random.permutation(order_key, pool_count)
    half_dev = R_DEV // 2
    imbalance = jax.random.randint(spread_key, (pool_count // 2,), 0, half_dev + 1)
    imbalance = imbalance.at[0].set(half_dev)
    owner_loads = R_DEV + jnp.stack([imbalance, -imbalance], axis=1).reshape(pool_count)
    run_ends = jnp.cumsum(owner_loads)
    positions = jnp.arange(R)
    run_index = jnp.sum((positions[:, None] >= run_ends[None, :]).astype(jnp.int32), axis=1)
    listed = owner_order[run_index]
    return listed[positions % R_DEV * pool_count + positions // R_DEV]


def offset_table(key, top):
    key = jax.random.fold_in(key, 202)
    return jax.random.uniform(key, (R, HEADS), jnp.float32, 0.0, top)


def forget_preactivation(key, leading_extent, sequence_length, rapid_fraction, spike_events):
    rapid_random_key, gradual_random_key, brisk_random_key, coarse_random_key, spike_random_key, location_random_key = jax.random.split(key, 6)
    fast_heads = jax.random.uniform(rapid_random_key, leading_extent) < rapid_fraction
    quick_rates = jnp.exp(jax.random.uniform(brisk_random_key, leading_extent, jnp.float32, math.log(0.02), math.log(0.035)))
    slow_rates = jnp.exp(jax.random.uniform(gradual_random_key, leading_extent, jnp.float32, math.log(0.0005), math.log(0.005)))
    decay_rates = jnp.where(fast_heads, quick_rates, slow_rates)
    amount_values = decay_rates[..., None] * jax.random.uniform(coarse_random_key, leading_extent + (sequence_length,), jnp.float32, 0.5, 1.5)
    if spike_events > 0:
        spike_positions = jax.random.randint(location_random_key, leading_extent + (spike_events,), 0, sequence_length)
        struck_flags = jnp.any(jnp.arange(sequence_length) == spike_positions[..., None], axis=-2)
        amount_values = jnp.where(struck_flags, jax.random.uniform(spike_random_key, leading_extent + (sequence_length,), jnp.float32, 0.3, 0.7), amount_values)
    return -jnp.log(jnp.expm1(amount_values))


def draw_owner_map(key, part):
    table = route_table(key)
    return table


def draw_prompt_len(key, part):
    key = jax.random.fold_in(key, 2)
    length_key, spot_key = jax.random.split(key)
    lengths = jax.random.randint(length_key, (R,), 1, BLOCK + 1)
    return lengths.at[jax.random.randint(spot_key, (), 0, R)].set(BLOCK)


def draw_stabilizer(key, part):
    top = 3.0
    offsets = offset_table(key, top)
    key = jax.random.fold_in(key, 3)
    return offsets + 4.0 + jax.random.truncated_normal(key, -4.0, 4.0, (R, HEADS), jnp.float32)


def draw_block_igate(key, part):
    top = 3.0
    offsets = offset_table(key, top)
    key = jax.random.fold_in(key, 4)
    return (offsets[:, :, None] + 2.0 * jax.random.truncated_normal(key, -4.0, 4.0, (R, HEADS, BLOCK), jnp.float32)).astype(jnp.bfloat16)


def draw_block_fgate(key, part):
    share = 0.5
    key = jax.random.fold_in(key, 5)
    return forget_preactivation(key, (R, HEADS), BLOCK, share, 2).astype(jnp.bfloat16)


def draw_step_igate(key, part):
    top = 3.0
    table = route_table(key)
    offsets = offset_table(key, top)
    key = jax.random.fold_in(key, 6)
    pool_count = R // R_DEV
    owners_hot = (table[:, None] == jnp.arange(pool_count)[None, :]).astype(jnp.int32)
    rank_in = jnp.sum((jnp.cumsum(owners_hot, axis=0) - owners_hot) * owners_hot, axis=1)
    target = table * CAP + rank_in
    request_of = jnp.zeros((SLOTS,), jnp.int32).at[target].set(jnp.arange(R))
    return (offsets[request_of][:, :, None] + 4.0 + 2.0 * jax.random.truncated_normal(key, -4.0, 4.0, (SLOTS, HEADS, STEPS), jnp.float32)).astype(jnp.bfloat16)


def draw_step_fgate(key, part):
    share = 0.5
    key = jax.random.fold_in(key, 7)
    return forget_preactivation(key, (SLOTS, HEADS), STEPS, share, 0).astype(jnp.bfloat16)


def shard_levels(own_key, extent, cuts, least, top_value):
    def one(dim, parts):
        draws = jax.random.uniform(jax.random.fold_in(jax.random.fold_in(own_key, 6), dim), (parts,), jnp.float32, least / len(cuts), top_value / len(cuts))
        return jnp.repeat(jnp.exp(draws), extent[dim] // parts).reshape((-1,) + (1,) * (len(extent) - dim - 1))

    loudness = one(*cuts[0])
    for cut in cuts[1:]:
        loudness = loudness * one(*cut)
    return loudness


def gaussian(key, shape, width, bound, shards=(), kind=jnp.bfloat16):
    values = width * jax.random.normal(key, shape, jnp.float32)
    if shards:
        values = values * shard_levels(key, shape, shards, -0.22, 0.18)
    return jnp.clip(values, -bound, bound).astype(kind)


def setup_inputs(seed: int = 0, part: int = 0) -> dict:
    key_of = jax.random.split(jax.random.key(seed), 17)
    part_keys = jax.random.split(jax.random.fold_in(key_of[16], part), 17)
    return {
        "owner_map": draw_owner_map(jax.random.fold_in(jax.random.fold_in(key_of[16], part), 71), part),
        "prompt_len": draw_prompt_len(jax.random.fold_in(jax.random.fold_in(key_of[16], part), 71), part),
        "memory": gaussian(part_keys[2], (R, HEADS, DQK, DV), 1.0, 6.0, ((0, 4), (1, 4))),
        "normalizer": jnp.clip(jnp.exp(math.log(3.0) - 1.0986123 * jax.random.uniform(part_keys[3], (R, HEADS, DQK), jnp.float32) ** shard_levels(part_keys[3], (R, HEADS, DQK), ((0, 4), (1, 4)), -0.2, 0.2)), 1.0, 3.0),
        "stabilizer": draw_stabilizer(jax.random.fold_in(jax.random.fold_in(key_of[16], part), 71), part),
        "block_q": jnp.clip(-1.0 + 3.0 * jax.random.uniform(part_keys[5], (R, BLOCK, HEADS * DQK), jnp.float32) ** shard_levels(part_keys[5], (R, BLOCK, HEADS * DQK), ((0, 4), (2, 4)), -0.2, 0.2), -1.0, 2.0).astype(jnp.bfloat16),
        "block_k": jnp.clip(-1.0 + 3.0 * jax.random.uniform(part_keys[6], (R, BLOCK, HEADS * DQK), jnp.float32) ** shard_levels(part_keys[6], (R, BLOCK, HEADS * DQK), ((0, 4), (2, 4)), -0.2, 0.2), -1.0, 2.0).astype(jnp.bfloat16),
        "block_v": gaussian(part_keys[7], (R, BLOCK, HEADS * DV), 1.0, 6.0, ((0, 4), (2, 4))),
        "block_igate": draw_block_igate(jax.random.fold_in(jax.random.fold_in(key_of[16], part), 71), part),
        "block_fgate": draw_block_fgate(jax.random.fold_in(jax.random.fold_in(key_of[16], part), 71), part),
        "step_q": jnp.clip(-1.0 + 3.0 * jax.random.uniform(part_keys[10], (SLOTS, STEPS, HEADS * DQK), jnp.float32) ** shard_levels(part_keys[10], (SLOTS, STEPS, HEADS * DQK), ((0, 4), (2, 4)), -0.2, 0.2), -1.0, 2.0).astype(jnp.bfloat16),
        "step_k": jnp.clip(-1.0 + 3.0 * jax.random.uniform(part_keys[11], (SLOTS, STEPS, HEADS * DQK), jnp.float32) ** shard_levels(part_keys[11], (SLOTS, STEPS, HEADS * DQK), ((0, 4), (2, 4)), -0.2, 0.2), -1.0, 2.0).astype(jnp.bfloat16),
        "step_v": gaussian(part_keys[12], (SLOTS, STEPS, HEADS * DV), 1.0, 6.0, ((0, 4), (2, 4))),
        "step_igate": draw_step_igate(jax.random.fold_in(jax.random.fold_in(key_of[16], part), 71), part),
        "step_fgate": draw_step_fgate(jax.random.fold_in(jax.random.fold_in(key_of[16], part), 71), part),
        "out_weight": gaussian(key_of[15], (HEADS * DV, D), (HEADS * DV) ** -0.5, 0.125, ((0, 4),)),
    }


HIGHEST = lax.Precision.HIGHEST

def prefill_one(queries, key_rows, value_rows, in_gates, forget_gates, memory, normalizer, stabilizer, sequence_length):
    head_count, qk_width, v_width = memory.shape
    block_len = queries.shape[0]
    scaling = 1.0 / math.sqrt(qk_width)
    query_full = queries.reshape(block_len, head_count, qk_width).astype(jnp.float32)
    key_full = key_rows.reshape(block_len, head_count, qk_width).astype(jnp.float32)
    value_full = value_rows.reshape(block_len, head_count, v_width).astype(jnp.float32)
    gate_in = in_gates.astype(jnp.float32)
    cumulated = jnp.cumsum(jax.nn.log_sigmoid(forget_gates.astype(jnp.float32)), axis=1)
    position = jnp.arange(block_len)
    causal = position[:, None] >= position[None, :]
    decays = cumulated[:, :, None] - cumulated[:, None, :] + gate_in[:, None, :]
    decays = jnp.where(causal[None], decays, -jnp.inf)
    carried = cumulated + stabilizer[:, None]
    running = jnp.maximum(carried, lax.optimization_barrier(jnp.max(decays, axis=2)))
    weights = jnp.exp(decays - running[:, :, None])
    retained = jnp.exp(carried - running)
    scores = jnp.einsum('thd,shd->hts', query_full, key_full, precision=HIGHEST) * scaling
    weighted = scores * weights
    mixing = lax.optimization_barrier(weighted.astype(jnp.bfloat16)).astype(jnp.float32)
    inner = jnp.einsum('hts,shv->thv', mixing, value_full, precision=HIGHEST)
    recalled = jnp.einsum('hdv,thd->thv', memory.astype(jnp.float32), query_full, precision=HIGHEST) * scaling
    numerator = retained.T[:, :, None] * recalled + inner
    normal_dot = jnp.einsum('hd,thd->th', normalizer, query_full, precision=HIGHEST) * scaling
    denominator = retained.T * normal_dot + lax.optimization_barrier(jnp.sum(weighted, axis=2)).T
    denominator = jnp.maximum(jnp.abs(denominator), jnp.exp(-running.T))
    outputs = numerator / denominator[:, :, None]
    outputs = jnp.where((position < sequence_length)[:, None, None], outputs, 0.0)
    selector = (position == sequence_length - 1).astype(jnp.float32)
    last_weights = lax.optimization_barrier(jnp.sum(selector[None, :, None] * weights, axis=1))
    last_kept = lax.optimization_barrier(jnp.sum(selector[None, :] * retained, axis=1))
    last_max = lax.optimization_barrier(jnp.sum(selector[None, :] * running, axis=1))
    weighted_keys = key_full * last_weights.T[:, :, None]
    memory_end = last_kept[:, None, None] * memory.astype(jnp.float32) + jnp.einsum('shd,shv->hdv', weighted_keys, value_full, precision=HIGHEST)
    normal_end = last_kept[:, None] * normalizer + lax.optimization_barrier(jnp.sum(weighted_keys, axis=0))
    return (outputs.reshape(block_len, head_count * v_width), memory_end, normal_end, last_max)

def decode_batch(memory, normalizer, stabilizer, queries, key_rows, value_rows, in_gates, forget_gates):
    batch_size, head_count, qk_width, v_width = memory.shape
    scaling = 1.0 / math.sqrt(qk_width)
    outputs = []
    for step_index in range(queries.shape[1]):
        query_now = queries[:, step_index].reshape(batch_size, head_count, qk_width).astype(jnp.float32) * scaling
        key_now = key_rows[:, step_index].reshape(batch_size, head_count, qk_width).astype(jnp.float32)
        value_now = value_rows[:, step_index].reshape(batch_size, head_count, v_width).astype(jnp.float32)
        log_forget = jax.nn.log_sigmoid(forget_gates[:, :, step_index].astype(jnp.float32))
        gate_in = in_gates[:, :, step_index].astype(jnp.float32)
        updated = jnp.maximum(log_forget + stabilizer, gate_in)
        retained = jnp.exp(log_forget + stabilizer - updated)
        admitted = jnp.exp(gate_in - updated)
        memory = retained[:, :, None, None] * memory + admitted[:, :, None, None] * key_now[:, :, :, None] * value_now[:, :, None, :]
        normalizer = retained[:, :, None] * normalizer + admitted[:, :, None] * key_now
        numerator = jnp.einsum('bhdv,bhd->bhv', memory, query_now, precision=HIGHEST)
        denominator = jnp.maximum(jnp.abs(lax.optimization_barrier(jnp.sum(normalizer * query_now, axis=2))), jnp.exp(-updated))
        outputs.append((numerator / denominator[:, :, None]).reshape(batch_size, head_count * v_width))
        stabilizer = updated
    return (jnp.stack(outputs, axis=1), memory, normalizer, stabilizer)

def project(hidden, weight):
    rounded = hidden.astype(jnp.bfloat16)
    share = rounded.shape[1] // N_TENSOR
    summed = jnp.zeros((rounded.shape[0], weight.shape[1]), jnp.float32)
    for part_index in range(N_TENSOR):
        term = jnp.dot(rounded[:, part_index * share:(part_index + 1) * share], weight[part_index * share:(part_index + 1) * share], preferred_element_type=jnp.float32)
        summed = summed + lax.optimization_barrier(term.astype(jnp.bfloat16)).astype(jnp.float32)
    return summed.astype(jnp.bfloat16)

def grouped(array, count):
    return array.reshape((count, array.shape[0] // count) + array.shape[1:])

def reference(owner_map, prompt_len, memory, normalizer, stabilizer, block_q, block_k, block_v, block_igate, block_fgate, step_q, step_k, step_v, step_igate, step_fgate, out_weight):

    def prefill_group(packed):
        return jax.vmap(prefill_one)(*packed)
    packed_in = tuple((grouped(item, N_POOL) for item in (block_q, block_k, block_v, block_igate, block_fgate, memory, normalizer, stabilizer, prompt_len)))
    block_hidden, memory_end, normal_end, max_end = lax.map(prefill_group, packed_in)
    block_hidden = block_hidden.reshape(R * BLOCK, -1)
    memory_end = memory_end.reshape((R,) + memory_end.shape[2:])
    normal_end = normal_end.reshape((R,) + normal_end.shape[2:])
    max_end = max_end.reshape((R,) + max_end.shape[2:])
    block_out = project(block_hidden, out_weight).reshape(R, BLOCK, D)
    owners_hot = (owner_map[:, None] == jnp.arange(N_POOL)[None, :]).astype(jnp.int32)
    rank_in = lax.optimization_barrier(jnp.sum((jnp.cumsum(owners_hot, axis=0) - owners_hot) * owners_hot, axis=1))
    target = owner_map * CAP + rank_in
    slot_memory = jnp.zeros((SLOTS,) + memory_end.shape[1:], memory_end.dtype).at[target].set(memory_end)
    slot_normal = jnp.zeros((SLOTS,) + normal_end.shape[1:], normal_end.dtype).at[target].set(normal_end)
    slot_max = jnp.zeros((SLOTS,) + max_end.shape[1:], max_end.dtype).at[target].set(max_end)
    filled = jnp.zeros((SLOTS,), jnp.int32).at[target].set(1)

    def decode_group(packed):
        return decode_batch(*packed)
    packed_slots = tuple((grouped(item, N_POOL) for item in (slot_memory, slot_normal, slot_max, step_q, step_k, step_v, step_igate, step_fgate)))
    step_hidden, memory_fin, normal_fin, max_fin = lax.map(decode_group, packed_slots)
    step_hidden = step_hidden.reshape((SLOTS,) + step_hidden.shape[2:])
    memory_fin = memory_fin.reshape((SLOTS,) + memory_fin.shape[2:])
    normal_fin = normal_fin.reshape((SLOTS,) + normal_fin.shape[2:])
    max_fin = max_fin.reshape((SLOTS,) + max_fin.shape[2:])
    live_mask = filled.astype(step_hidden.dtype)
    step_hidden = step_hidden * live_mask[:, None, None]
    step_out = project(step_hidden.reshape(SLOTS * STEPS, -1), out_weight).reshape(SLOTS, STEPS, D)
    memory_out = (memory_fin * live_mask[:, None, None, None]).astype(jnp.bfloat16)
    normalizer_out = normal_fin * live_mask[:, None, None]
    max_out = max_fin * live_mask[:, None]
    return (block_out, step_out, memory_out, normalizer_out, max_out)
```

```python
import functools
import math

import jax
import jax.numpy as jnp
from jax import lax
from jax.experimental import pallas as pl
from jax.experimental.pallas import tpu as pltpu
from jax.sharding import PartitionSpec as P

F32 = jnp.float32
BF16 = jnp.bfloat16
HIGHEST = lax.Precision.HIGHEST
MESH = pl.DeviceIdType.MESH
VMEM_LIMIT = 40 * 1024 * 1024


def gate_terms(igate, fgate, start):
    count = igate.shape[1]
    position = jnp.arange(count)
    causal = (position[:, None] >= position[None, :])[None]
    log_forget = jax.nn.log_sigmoid(fgate.astype(F32))
    summed = jnp.sum(jnp.where(causal, log_forget[:, None, :], 0.0), axis=2)
    decays = summed[:, :, None] - summed[:, None, :] + igate.astype(F32)[:, None, :]
    decays = jnp.where(causal, decays, -jnp.inf)
    carried = summed + start[:, None]
    running = jnp.maximum(carried, jnp.max(decays, axis=2))
    weights = jnp.exp(decays - running[:, :, None])
    retained = jnp.exp(carried - running)
    return weights, retained, running


def divisor(count, most):
    return max(d for d in range(1, most + 1) if count % d == 0)


def pack_kernel(group, send_from, kept, *refs):
    memories, keys, values, out = refs[:group], refs[group : 2 * group], refs[2 * group : -1], refs[-1]
    step = pl.program_id(0)
    for g in range(group):
        keep = kept[send_from[step * group + g]]
        outer = lax.dot_general(
            keys[g][0], values[g][0], (((0,), (0,)), ((), ())), preferred_element_type=F32
        )
        out[g] = (memories[g][0].astype(F32) * keep + outer).astype(BF16)


def pack_states(send_from, kept, memory, weighted_keys, values):
    slots = send_from.shape[0]
    group = divisor(slots, 4)
    block, dqk = weighted_keys.shape[1:]
    dv = values.shape[2]

    def spec(shape, g):
        return pl.BlockSpec(
            (1,) + shape, lambda i, pick, kept: (pick[i * group + g], 0, 0)
        )

    in_specs = (
        [spec((dqk, dv), g) for g in range(group)]
        + [spec((block, dqk), g) for g in range(group)]
        + [spec((block, dv), g) for g in range(group)]
    )
    return pl.pallas_call(
        functools.partial(pack_kernel, group),
        out_shape=jax.ShapeDtypeStruct((slots, dqk, dv), BF16),
        grid_spec=pltpu.PrefetchScalarGridSpec(
            num_scalar_prefetch=2,
            grid=(slots // group,),
            in_specs=in_specs,
            out_specs=pl.BlockSpec((group, dqk, dv), lambda i, pick, kept: (i, 0, 0)),
        ),
        compiler_params=pltpu.CompilerParams(vmem_limit_bytes=VMEM_LIMIT),
        cost_estimate=pl.CostEstimate(
            flops=2 * slots * block * dqk * dv, bytes_accessed=4 * slots * dqk * dv, transcendentals=0
        ),
    )(send_from, kept, *([memory] * group), *([weighted_keys] * group), *([values] * group))


def decode_kernel(group, steps, pick, last_kept, *refs):
    memories = refs[:group]
    queries, keys, values, alpha, inner, _, memory_out, hidden = refs[group:]
    step = pl.program_id(0)

    @pl.when(step == 0)
    def _():
        hidden[...] = jnp.zeros_like(hidden)

    rows = []
    for g in range(group):
        state = memories[g][0]
        recalled = jnp.dot(queries[g], state, preferred_element_type=F32)
        rows.append((alpha[g] * recalled + inner[g])[:steps])
        outer = lax.dot_general(
            keys[g], values[g], (((0,), (0,)), ((), ())), preferred_element_type=F32
        )
        keep = last_kept[step * group + g]
        memory_out[g] = (state.astype(F32) * keep + outer).astype(BF16)
    taken = group * steps
    hidden[pl.ds(pl.multiple_of(step * taken, taken), taken), :] = jnp.concatenate(rows, axis=0)


def decode_states(pick, last_kept, arrived, queries, keys, values, alpha, inner, after, steps):
    slots, padded, dqk = queries.shape
    dv = values.shape[2]
    group = divisor(slots, 6)
    rows = -(-slots * steps // 16) * 16

    def spec(g):
        return pl.BlockSpec((1, dqk, dv), lambda i, pick, kept: (pick[i * group + g], 0, 0))

    def part(width):
        return pl.BlockSpec((group, padded, width), lambda i, pick, kept: (i, 0, 0))

    return pl.pallas_call(
        functools.partial(decode_kernel, group, steps),
        out_shape=(
            jax.ShapeDtypeStruct((slots, dqk, dv), BF16),
            jax.ShapeDtypeStruct((rows, dv), F32),
        ),
        grid_spec=pltpu.PrefetchScalarGridSpec(
            num_scalar_prefetch=2,
            grid=(slots // group,),
            in_specs=[spec(g) for g in range(group)]
            + [part(dqk), part(dqk), part(dv), part(1), part(dv)]
            + [pl.BlockSpec(memory_space=pl.ANY)],
            out_specs=(
                pl.BlockSpec((group, dqk, dv), lambda i, pick, kept: (i, 0, 0)),
                pl.BlockSpec((rows, dv), lambda i, pick, kept: (0, 0)),
            ),
        ),
        compiler_params=pltpu.CompilerParams(vmem_limit_bytes=VMEM_LIMIT),
        cost_estimate=pl.CostEstimate(
            flops=4 * slots * padded * dqk * dv, bytes_accessed=4 * slots * dqk * dv, transcendentals=0
        ),
    )(pick, last_kept, *([arrived] * group), queries, keys, values, alpha, inner, after)


def project_kernel(axis, count, hidden, weight, out, sent, held, send_sem, recv_sem):
    me = lax.axis_index(axis)
    width = out.shape[1]
    barrier = pltpu.get_barrier_semaphore()
    for k in range(1, count):
        pl.semaphore_signal(
            barrier, inc=1, device_id={axis: lax.rem(me + k, count)}, device_id_type=MESH
        )
    rounded = hidden[...].astype(BF16)

    def product(owner):
        columns = pl.ds(pl.multiple_of(owner * width, width), width)
        return jnp.dot(rounded, weight[:, columns], preferred_element_type=F32).astype(BF16)

    copies = []
    for k in range(1, count):
        target = lax.rem(me + k, count)
        sent[k - 1] = product(target)
        if k == 1:
            pl.semaphore_wait(barrier, count - 1)
        copy = pltpu.make_async_remote_copy(
            src_ref=sent.at[k - 1],
            dst_ref=held.at[k - 1],
            send_sem=send_sem.at[k - 1],
            recv_sem=recv_sem.at[k - 1],
            device_id={axis: target},
            device_id_type=MESH,
        )
        copy.start()
        copies.append(copy)
    total = product(me).astype(F32)
    for k in range(1, count):
        copies[k - 1].wait_recv()
        total = total + held[k - 1].astype(F32)
    out[...] = total.astype(BF16)
    for copy in copies:
        copy.wait_send()


def project_sum(hidden, weight, axis, collective_id):
    count = lax.axis_size(axis)
    rows = hidden.shape[0]
    width = weight.shape[1] // count
    vmem = pl.BlockSpec(memory_space=pltpu.VMEM)
    return pl.pallas_call(
        functools.partial(project_kernel, axis, count),
        out_shape=jax.ShapeDtypeStruct((rows, width), BF16),
        in_specs=[vmem, vmem],
        out_specs=vmem,
        scratch_shapes=[
            pltpu.VMEM((count - 1, rows, width), BF16),
            pltpu.VMEM((count - 1, rows, width), BF16),
            pltpu.SemaphoreType.DMA((count - 1,)),
            pltpu.SemaphoreType.DMA((count - 1,)),
        ],
        compiler_params=pltpu.CompilerParams(
            collective_id=collective_id, has_side_effects=True, vmem_limit_bytes=VMEM_LIMIT
        ),
        cost_estimate=pl.CostEstimate(
            flops=2 * rows * weight.size,
            bytes_accessed=2 * weight.size,
            transcendentals=0,
        ),
    )(hidden, weight)


def body(
    owner_map,
    prompt_len,
    memory,
    normalizer,
    stabilizer,
    block_q,
    block_k,
    block_v,
    block_igate,
    block_fgate,
    step_q,
    step_k,
    step_v,
    step_igate,
    step_fgate,
    out_weight,
):
    pool_size = lax.axis_size("pool")
    my_index = lax.axis_index("pool")
    requests, block = block_q.shape[:2]
    dqk, dv = memory.shape[2:]
    slots, steps = step_q.shape[:2]
    capacity = requests + requests // 2
    pair_cap = (capacity + pool_size - 1) // pool_size
    buffer_len = pool_size * pair_cap
    scaling = 1.0 / math.sqrt(dqk)
    memory = memory.reshape(requests, dqk, dv)
    normalizer = normalizer.reshape(requests, dqk)
    block_igate, block_fgate = block_igate[:, 0], block_fgate[:, 0]
    step_igate, step_fgate = step_igate[:, 0], step_fgate[:, 0]

    own_rows = lax.dynamic_slice_in_dim(owner_map, my_index * requests, requests)
    ids = jnp.arange(requests)
    earlier = (own_rows[:, None] == own_rows[None, :]) & (ids[:, None] > ids[None, :])
    send_slot = own_rows * pair_cap + jnp.sum(earlier.astype(jnp.int32), axis=1)
    slot_hits = send_slot[None, :] == jnp.arange(buffer_len)[:, None]
    send_from = jnp.sum(jnp.where(slot_hits, ids[None, :], 0), axis=1)

    weights, retained, running = gate_terms(block_igate, block_fgate, stabilizer[:, 0])
    last = jnp.arange(block)[None, :] == prompt_len[:, None] - 1
    last_weights = jnp.sum(jnp.where(last[:, :, None], weights, 0.0), axis=1)
    last_kept = jnp.sum(jnp.where(last, retained, 0.0), axis=1)
    last_max = jnp.sum(jnp.where(last, running, 0.0), axis=1)
    weighted_keys = block_k.astype(F32) * last_weights[:, :, None]
    packed = pack_states(send_from, last_kept, memory, weighted_keys.astype(BF16), block_v)
    arrived = lax.all_to_all(packed, "pool", split_axis=0, concat_axis=0, tiled=True)
    normal_end = last_kept[:, None] * normalizer + jnp.sum(weighted_keys, axis=1)
    small = jnp.concatenate(
        [normal_end, jnp.broadcast_to(last_max[:, None], (requests, 128))], axis=1
    )
    small = lax.all_gather(small, "pool", axis=0, tiled=True)

    scores = jnp.einsum("ntd,nsd->nts", block_q, block_k, preferred_element_type=F32) * scaling
    weighted = scores * weights
    inner = jnp.einsum("nts,nsv->ntv", weighted.astype(BF16), block_v, preferred_element_type=F32)
    recalled = jnp.einsum("ntd,ndv->ntv", block_q, memory, preferred_element_type=F32) * scaling
    normal_dot = jnp.sum(normalizer[:, None, :] * block_q.astype(F32), axis=2) * scaling
    denominator = jnp.maximum(
        jnp.abs(retained * normal_dot + jnp.sum(weighted, axis=2)), jnp.exp(-running)
    )
    block_hidden = (retained[:, :, None] * recalled + inner) / denominator[:, :, None]
    used = jnp.arange(block)[None, :] < prompt_len[:, None]
    block_hidden = jnp.where(used[:, :, None], block_hidden, 0.0).astype(BF16)
    block_terms = jnp.dot(
        block_hidden.reshape(requests * block, dv), out_weight, preferred_element_type=F32
    ).astype(BF16)
    block_out = lax.psum_scatter(block_terms, "tensor", scatter_dimension=1, tiled=True)

    everyone = jnp.arange(owner_map.shape[0])
    before = everyone[:, None] > everyone[None, :]
    mine = owner_map == my_index
    same_source = (everyone[:, None] // requests) == (everyone[None, :] // requests)
    rank = jnp.sum((before & mine[None, :]).astype(jnp.int32), axis=1)
    pair_rank = jnp.sum((before & same_source & mine[None, :]).astype(jnp.int32), axis=1)
    takes = mine[None, :] & (rank[None, :] == jnp.arange(slots)[:, None])
    request_of = jnp.sum(jnp.where(takes, everyone[None, :], 0), axis=1)
    landed = (everyone // requests) * pair_cap + pair_rank
    gather_from = jnp.sum(jnp.where(takes, landed[None, :], 0), axis=1)
    live = jnp.any(takes, axis=1)

    start = jnp.take(small, request_of, axis=0)
    start_normal, start_max = start[:, :dqk], start[:, dqk]
    weights, retained, running = gate_terms(step_igate, step_fgate, start_max)
    scores = jnp.einsum("ntd,nsd->nts", step_q, step_k, preferred_element_type=F32) * scaling
    weighted = scores * weights
    normal_dot = jnp.sum(start_normal[:, None, :] * step_q.astype(F32), axis=2) * scaling
    denominator = jnp.maximum(
        jnp.abs(retained * normal_dot + jnp.sum(weighted, axis=2)), jnp.exp(-running)
    )
    value_rows = step_v.astype(F32)
    inner = jnp.sum(weighted[:, :, :, None] * value_rows[:, None, :, :], axis=2)
    inner = jnp.where(live[:, None, None], inner / denominator[:, :, None], 0.0)
    alpha = jnp.where(live[:, None], retained * scaling / denominator, 0.0)
    step_keys = jnp.where(
        live[:, None, None], step_k.astype(F32) * weights[:, steps - 1, :, None], 0.0
    )
    step_kept = jnp.where(live, retained[:, steps - 1], 0.0)
    normalizer_out = step_kept[:, None] * start_normal + jnp.sum(step_keys, axis=1)
    max_out = jnp.where(live, running[:, steps - 1], 0.0)

    def pad(array):
        return jnp.pad(array, ((0, 0), (0, -steps % 16), (0, 0)))

    memory_out, step_hidden = decode_states(
        gather_from,
        step_kept,
        arrived,
        pad(step_q),
        pad(step_keys.astype(BF16)),
        pad(step_v),
        pad(alpha[:, :, None]),
        pad(inner),
        block_out,
        steps,
    )
    step_out = project_sum(step_hidden, out_weight, "tensor", 1)[: slots * steps]
    return (
        block_out.reshape(requests, block, -1),
        step_out.reshape(slots, steps, -1),
        memory_out[:, None],
        normalizer_out[:, None],
        max_out[:, None],
    )


def solution(mesh):
    rows = ("group", "pool")
    return jax.shard_map(
        body,
        mesh=mesh,
        in_specs=(
            P("group"),
            P(rows),
            P(rows, "tensor", None, None),
            P(rows, "tensor", None),
            P(rows, "tensor"),
            P(rows, None, "tensor"),
            P(rows, None, "tensor"),
            P(rows, None, "tensor"),
            P(rows, "tensor", None),
            P(rows, "tensor", None),
            P(rows, None, "tensor"),
            P(rows, None, "tensor"),
            P(rows, None, "tensor"),
            P(rows, "tensor", None),
            P(rows, "tensor", None),
            P("tensor", None),
        ),
        out_specs=(
            P(rows, None, "tensor"),
            P(rows, None, "tensor"),
            P(rows, "tensor", None, None),
            P(rows, "tensor", None),
            P(rows, "tensor"),
        ),
        check_vma=False,
    )
```

```python
import functools
import math

import jax
import jax.numpy as jnp
from jax import lax
from jax.experimental import pallas as pl
from jax.experimental.pallas import tpu as pltpu
from jax.sharding import PartitionSpec as P

F32 = jnp.float32
BF16 = jnp.bfloat16
MESH = pl.DeviceIdType.MESH
VMEM_LIMIT = 40 * 1024 * 1024


def gate_terms(igate, fgate, start):
    count = igate.shape[2]
    row = lax.broadcasted_iota(jnp.int32, (1, count, count), 1)
    column = lax.broadcasted_iota(jnp.int32, (1, count, count), 2)
    log_forget = jnp.minimum(fgate, 0.0) - jnp.log(1.0 + jnp.exp(-jnp.abs(fgate)))
    summed = jnp.sum(jnp.where(row >= column, log_forget, 0.0), axis=2, keepdims=True)
    across = jnp.sum(jnp.where(row == column, summed, 0.0), axis=1, keepdims=True)
    decays = jnp.where(row >= column, summed - across + igate, -jnp.inf)
    carried = summed + start
    running = jnp.maximum(carried, jnp.max(decays, axis=2, keepdims=True))
    weights = jnp.exp(decays - running)
    retained = jnp.exp(carried - running)
    return weights, retained, running


def as_column(rows):
    count = rows.shape[2]
    row = lax.broadcasted_iota(jnp.int32, (1, count, count), 1)
    column = lax.broadcasted_iota(jnp.int32, (1, count, count), 2)
    return jnp.sum(jnp.where(row == column, rows, 0.0), axis=2, keepdims=True)


def divisor(count, most):
    return max(d for d in range(1, most + 1) if count % d == 0)


def send_order(count):
    far = count // 2
    return sorted(range(1, count), key=lambda k: (abs(k - far), k))


def exchange_kernel(pool, heads, pair_cap, padded, *refs):
    (
        send_from, request_of,
        length, igate, fgate, start, normalizer, memory, queries, keys, values,
        step_igate, step_fgate, live, step_q, step_k, step_v, weight,
        arrived, block_out, alpha_out, inner_out, query_out, key_out, value_out,
        normalizer_out, max_out,
        weights_s, retained_s, floor_s, used_s, keys_s, kept_s, small_s, begin_s, sent,
        hidden_s, weight_s, part_sent, part_held,
        small_send, small_recv, slot_send, slot_recv, part_send, part_recv, own_sem, weight_sem,
    ) = refs
    axis_p, count_p = pool
    axis_t, count_t = heads
    me = lax.axis_index(axis_p)
    mine = lax.axis_index(axis_t)
    requests, block, dqk = keys.shape
    dv = values.shape[2]
    slots, steps = step_q.shape[:2]
    width = block_out.shape[1]
    scaling = 1.0 / math.sqrt(dqk)

    load_weight = pltpu.make_async_copy(weight, weight_s, weight_sem)
    load_weight.start()
    barrier = pltpu.get_barrier_semaphore()
    for k in range(1, count_p):
        pl.semaphore_signal(
            barrier, inc=1, device_id={axis_p: lax.rem(me + k, count_p)}, device_id_type=MESH
        )
    for k in range(1, count_t):
        pl.semaphore_signal(
            barrier, inc=1, device_id={axis_t: lax.rem(mine + k, count_t)}, device_id_type=MESH
        )

    weights, retained, running = gate_terms(igate[...], fgate[...], start[...])
    position = lax.broadcasted_iota(jnp.int32, (1, block, 1), 1)
    last = position == length[...] - 1
    last_weights = jnp.sum(jnp.where(last, weights, 0.0), axis=1, keepdims=True)
    last_kept = jnp.sum(jnp.where(last, retained, 0.0), axis=1, keepdims=True)
    last_max = jnp.sum(jnp.where(last, running, 0.0), axis=1, keepdims=True)
    weighted_keys = keys[...].astype(F32) * as_column(last_weights)
    keys_s[...] = weighted_keys.astype(BF16)
    kept_s[...] = jnp.broadcast_to(last_kept, (requests, 1, dv))
    weights_s[...] = weights * scaling
    retained_s[...] = retained
    floor_s[...] = jnp.exp(-running)
    used_s[...] = jnp.where(position < length[...], 1.0, 0.0)
    own = pl.ds(me * requests, requests)
    small_s[own, :, :dqk] = last_kept * normalizer[...] + jnp.sum(
        weighted_keys, axis=1, keepdims=True
    )
    small_s[own, :, dqk:] = jnp.broadcast_to(last_max, (requests, 1, 128))

    pl.semaphore_wait(barrier, count_p + count_t - 2)
    small_copies = []
    for k in range(1, count_p):
        copy = pltpu.make_async_remote_copy(
            src_ref=small_s.at[own],
            dst_ref=small_s.at[own],
            send_sem=small_send.at[k - 1],
            recv_sem=small_recv.at[k - 1],
            device_id={axis_p: lax.rem(me + k, count_p)},
            device_id_type=MESH,
        )
        copy.start()
        small_copies.append(copy)

    def pack(owner, place, j):
        index = send_from[owner * pair_cap + j]
        outer = lax.dot_general(
            keys_s[index], values[index], (((0,), (0,)), ((), ())), preferred_element_type=F32
        )
        sent[place, j] = (memory[index].astype(F32) * kept_s[index] + outer).astype(BF16)

    slot_copies = []
    for j in range(pair_cap):
        for k in send_order(count_p):
            target = lax.rem(me + k, count_p)
            pack(target, k, j)
            copy = pltpu.make_async_remote_copy(
                src_ref=sent.at[k, j],
                dst_ref=arrived.at[me * pair_cap + j],
                send_sem=slot_send.at[k - 1, j],
                recv_sem=slot_recv.at[k - 1, j],
                device_id={axis_p: target},
                device_id_type=MESH,
            )
            copy.start()
            slot_copies.append(copy)
    for j in range(pair_cap):
        pack(me, 0, j)
    keep_own = pltpu.make_async_copy(
        sent.at[0], arrived.at[pl.ds(me * pair_cap, pair_cap)], own_sem
    )
    keep_own.start()

    @pl.loop(0, requests)
    def _(i):
        query, value = queries[i], values[i]
        scores = lax.dot_general(
            query, keys[i], (((1,), (1,)), ((), ())), preferred_element_type=F32
        )
        weighted = scores * weights_s[i]
        total = jnp.dot(weighted.astype(BF16), value, preferred_element_type=F32)
        recalled = jnp.dot(query, memory[i], preferred_element_type=F32)
        dots = jnp.sum(query.astype(F32) * normalizer[i], axis=1, keepdims=True)
        kept = retained_s[i] * scaling
        denominator = kept * dots + jnp.sum(weighted, axis=1, keepdims=True)
        denominator = jnp.maximum(jnp.abs(denominator), floor_s[i])
        result = (kept * recalled + total) / denominator
        result = jnp.where(used_s[i] > 0.0, result, 0.0)
        hidden_s[pl.ds(pl.multiple_of(i * block, block), block), :] = result.astype(BF16)

    load_weight.wait()

    def product(owner):
        columns = pl.ds(pl.multiple_of(owner * width, width), width)
        return jnp.dot(hidden_s[...], weight_s[:, columns], preferred_element_type=F32).astype(BF16)

    part_copies = []
    for k in range(1, count_t):
        target = lax.rem(mine + k, count_t)
        part_sent[k - 1] = product(target)
        copy = pltpu.make_async_remote_copy(
            src_ref=part_sent.at[k - 1],
            dst_ref=part_held.at[k - 1],
            send_sem=part_send.at[k - 1],
            recv_sem=part_recv.at[k - 1],
            device_id={axis_t: target},
            device_id_type=MESH,
        )
        copy.start()
        part_copies.append(copy)
    summed = product(mine).astype(F32)
    for k in range(1, count_t):
        part_copies[k - 1].wait_recv()
        summed = summed + part_held[k - 1].astype(F32)
    block_out[...] = summed.astype(BF16)

    for copy in small_copies:
        copy.wait_recv()
    for s in range(slots):
        begin_s[s] = small_s[request_of[s]]
    begin_normal = begin_s[:, :, :dqk]
    begin_max = begin_s[:, :, dqk : dqk + 1]
    alive = live[...] > 0
    weights, retained, running = gate_terms(step_igate[...], step_fgate[...], begin_max)
    query = step_q[...].astype(F32)
    key = step_k[...].astype(F32)
    value = step_v[...].astype(F32)
    dots = jnp.sum(query * begin_normal, axis=2, keepdims=True)
    denominator = retained * dots
    inner = jnp.zeros(value.shape, F32)
    for s in range(steps):
        scores = jnp.sum(query * key[:, s : s + 1, :], axis=2, keepdims=True)
        weighted = scores * weights[:, :, s : s + 1]
        denominator = denominator + weighted
        inner = inner + weighted * value[:, s : s + 1, :]
    denominator = jnp.maximum(jnp.abs(denominator * scaling), jnp.exp(-running))
    inner = jnp.where(alive, inner * scaling / denominator, 0.0)
    alpha = jnp.where(alive, retained * scaling / denominator, 0.0)
    last_row = slice(steps - 1, steps)
    step_keys = jnp.where(alive, key * as_column(weights[:, last_row, :]), 0.0)
    kept = jnp.where(alive, retained[:, last_row, :], 0.0)
    normalizer_out[...] = kept * begin_normal + jnp.sum(step_keys, axis=1, keepdims=True)
    max_out[...] = jnp.where(alive, running[:, last_row, :], 0.0)

    def pad(array):
        blank = jnp.zeros((slots, padded - steps, array.shape[2]), F32)
        return jnp.concatenate([array, blank], axis=1)

    query_out[...] = pad(query).astype(BF16)
    key_out[...] = pad(step_keys).astype(BF16)
    value_out[...] = pad(value).astype(BF16)
    inner_out[...] = pad(inner)
    blank = jnp.zeros((slots, padded - steps - 1, 1), F32)
    columns = jnp.concatenate([alpha, kept, blank], axis=1)
    alpha_out[...] = jnp.broadcast_to(columns, (slots, padded, 128))

    keep_own.wait()
    for copy in part_copies:
        copy.wait_send()
    for copy in small_copies:
        copy.wait_send()
    for copy in slot_copies:
        copy.wait()


def exchange(arrays, pair_cap, padded, collective_id):
    memory, values, step_q, weight = arrays[7], arrays[10], arrays[14], arrays[17]
    requests, dqk, dv = memory.shape
    block = values.shape[1]
    slots = step_q.shape[0]
    count_p, count_t = lax.axis_size("pool"), lax.axis_size("tensor")
    rows, width = requests * block, weight.shape[1] // count_t
    smem = pl.BlockSpec(memory_space=pltpu.SMEM)
    vmem = pl.BlockSpec(memory_space=pltpu.VMEM)
    anywhere = pl.BlockSpec(memory_space=pl.ANY)
    dma = pltpu.SemaphoreType.DMA
    shape = jax.ShapeDtypeStruct
    return pl.pallas_call(
        functools.partial(
            exchange_kernel, ("pool", count_p), ("tensor", count_t), pair_cap, padded
        ),
        out_shape=(
            shape((count_p * pair_cap, dqk, dv), BF16),
            shape((rows, width), BF16),
            shape((slots, padded, 128), F32),
            shape((slots, padded, dv), F32),
            shape((slots, padded, dqk), BF16),
            shape((slots, padded, dqk), BF16),
            shape((slots, padded, dv), BF16),
            shape((slots, 1, dqk), F32),
            shape((slots, 1, 1), F32),
        ),
        in_specs=[smem] * 2 + [vmem] * 15 + [anywhere],
        out_specs=(anywhere,) + (vmem,) * 8,
        scratch_shapes=[
            pltpu.VMEM((requests, block, block), F32),
            pltpu.VMEM((requests, block, 1), F32),
            pltpu.VMEM((requests, block, 1), F32),
            pltpu.VMEM((requests, block, 1), F32),
            pltpu.VMEM((requests, block, dqk), BF16),
            pltpu.VMEM((requests, 1, dv), F32),
            pltpu.VMEM((count_p * requests, 1, dqk + 128), F32),
            pltpu.VMEM((slots, 1, dqk + 128), F32),
            pltpu.VMEM((count_p, pair_cap, dqk, dv), BF16),
            pltpu.VMEM((rows, dv), BF16),
            pltpu.VMEM(weight.shape, BF16),
            pltpu.VMEM((count_t - 1, rows, width), BF16),
            pltpu.VMEM((count_t - 1, rows, width), BF16),
            dma((count_p - 1,)),
            dma((count_p - 1,)),
            dma((count_p - 1, pair_cap)),
            dma((count_p - 1, pair_cap)),
            dma((count_t - 1,)),
            dma((count_t - 1,)),
            dma,
            dma,
        ],
        compiler_params=pltpu.CompilerParams(
            collective_id=collective_id, has_side_effects=True, vmem_limit_bytes=VMEM_LIMIT
        ),
    )(*arrays)


def decode_kernel(group, steps, pick, *refs):
    memories = refs[:group]
    queries, keys, values, alpha, inner, memory_out, hidden = refs[group:]
    step = pl.program_id(0)

    @pl.when(step == 0)
    def _():
        hidden[...] = jnp.zeros_like(hidden)

    rows = []
    for g in range(group):
        state = memories[g][0]
        recalled = jnp.dot(queries[g], state, preferred_element_type=F32)
        rows.append((alpha[g][:, :1] * recalled + inner[g])[:steps])
        outer = lax.dot_general(
            keys[g], values[g], (((0,), (0,)), ((), ())), preferred_element_type=F32
        )
        keep = alpha[g][steps : steps + 1, :1]
        memory_out[g] = (state.astype(F32) * keep + outer).astype(BF16)
    taken = group * steps
    hidden[pl.ds(pl.multiple_of(step * taken, taken), taken), :] = jnp.concatenate(rows, axis=0)


def decode_states(pick, arrived, queries, keys, values, alpha, inner, steps):
    slots, padded, dqk = queries.shape
    dv = values.shape[2]
    group = divisor(slots, 6)
    rows = -(-slots * steps // 16) * 16

    def spec(g):
        return pl.BlockSpec((1, dqk, dv), lambda i, pick: (pick[i * group + g], 0, 0))

    def part(width):
        return pl.BlockSpec((group, padded, width), lambda i, pick: (i, 0, 0))

    return pl.pallas_call(
        functools.partial(decode_kernel, group, steps),
        out_shape=(
            jax.ShapeDtypeStruct((slots, dqk, dv), BF16),
            jax.ShapeDtypeStruct((rows, dv), F32),
        ),
        grid_spec=pltpu.PrefetchScalarGridSpec(
            num_scalar_prefetch=1,
            grid=(slots // group,),
            in_specs=[spec(g) for g in range(group)]
            + [part(dqk), part(dqk), part(dv), part(128), part(dv)],
            out_specs=(
                pl.BlockSpec((group, dqk, dv), lambda i, pick: (i, 0, 0)),
                pl.BlockSpec((rows, dv), lambda i, pick: (0, 0)),
            ),
        ),
        compiler_params=pltpu.CompilerParams(vmem_limit_bytes=VMEM_LIMIT),
        cost_estimate=pl.CostEstimate(
            flops=4 * slots * padded * dqk * dv, bytes_accessed=4 * slots * dqk * dv, transcendentals=0
        ),
    )(pick, *([arrived] * group), queries, keys, values, alpha, inner)


def project_kernel(axis, count, hidden, weight, out, sent, held, send_sem, recv_sem):
    me = lax.axis_index(axis)
    width = out.shape[1]
    barrier = pltpu.get_barrier_semaphore()
    for k in range(1, count):
        pl.semaphore_signal(
            barrier, inc=1, device_id={axis: lax.rem(me + k, count)}, device_id_type=MESH
        )
    rounded = hidden[...].astype(BF16)

    def product(owner):
        columns = pl.ds(pl.multiple_of(owner * width, width), width)
        return jnp.dot(rounded, weight[:, columns], preferred_element_type=F32).astype(BF16)

    copies = []
    for k in range(1, count):
        target = lax.rem(me + k, count)
        sent[k - 1] = product(target)
        if k == 1:
            pl.semaphore_wait(barrier, count - 1)
        copy = pltpu.make_async_remote_copy(
            src_ref=sent.at[k - 1],
            dst_ref=held.at[k - 1],
            send_sem=send_sem.at[k - 1],
            recv_sem=recv_sem.at[k - 1],
            device_id={axis: target},
            device_id_type=MESH,
        )
        copy.start()
        copies.append(copy)
    total = product(me).astype(F32)
    for k in range(1, count):
        copies[k - 1].wait_recv()
        total = total + held[k - 1].astype(F32)
    out[...] = total.astype(BF16)
    for copy in copies:
        copy.wait_send()


def project_sum(hidden, weight, axis, collective_id):
    count = lax.axis_size(axis)
    rows = hidden.shape[0]
    width = weight.shape[1] // count
    vmem = pl.BlockSpec(memory_space=pltpu.VMEM)
    return pl.pallas_call(
        functools.partial(project_kernel, axis, count),
        out_shape=jax.ShapeDtypeStruct((rows, width), BF16),
        in_specs=[vmem, vmem],
        out_specs=vmem,
        scratch_shapes=[
            pltpu.VMEM((count - 1, rows, width), BF16),
            pltpu.VMEM((count - 1, rows, width), BF16),
            pltpu.SemaphoreType.DMA((count - 1,)),
            pltpu.SemaphoreType.DMA((count - 1,)),
        ],
        compiler_params=pltpu.CompilerParams(
            collective_id=collective_id, has_side_effects=True, vmem_limit_bytes=VMEM_LIMIT
        ),
        cost_estimate=pl.CostEstimate(
            flops=2 * rows * weight.size,
            bytes_accessed=2 * weight.size,
            transcendentals=0,
        ),
    )(hidden, weight)


def body(
    owner_map,
    prompt_len,
    memory,
    normalizer,
    stabilizer,
    block_q,
    block_k,
    block_v,
    block_igate,
    block_fgate,
    step_q,
    step_k,
    step_v,
    step_igate,
    step_fgate,
    out_weight,
):
    pool_size = lax.axis_size("pool")
    my_index = lax.axis_index("pool")
    requests, block = block_q.shape[:2]
    dqk, dv = memory.shape[2:]
    slots, steps = step_q.shape[:2]
    capacity = requests + requests // 2
    pair_cap = (capacity + pool_size - 1) // pool_size
    buffer_len = pool_size * pair_cap
    memory = memory.reshape(requests, dqk, dv)

    own_rows = lax.dynamic_slice_in_dim(owner_map, my_index * requests, requests)
    ids = jnp.arange(requests)
    earlier = (own_rows[:, None] == own_rows[None, :]) & (ids[:, None] > ids[None, :])
    send_slot = own_rows * pair_cap + jnp.sum(earlier.astype(jnp.int32), axis=1)
    slot_hits = send_slot[None, :] == jnp.arange(buffer_len)[:, None]
    send_from = jnp.sum(jnp.where(slot_hits, ids[None, :], 0), axis=1)

    everyone = jnp.arange(owner_map.shape[0])
    before = everyone[:, None] > everyone[None, :]
    mine = owner_map == my_index
    same_source = (everyone[:, None] // requests) == (everyone[None, :] // requests)
    rank = jnp.sum((before & mine[None, :]).astype(jnp.int32), axis=1)
    pair_rank = jnp.sum((before & same_source & mine[None, :]).astype(jnp.int32), axis=1)
    takes = mine[None, :] & (rank[None, :] == jnp.arange(slots)[:, None])
    request_of = jnp.sum(jnp.where(takes, everyone[None, :], 0), axis=1)
    landed = (everyone // requests) * pair_cap + pair_rank
    gather_from = jnp.sum(jnp.where(takes, landed[None, :], 0), axis=1)
    live = jnp.any(takes, axis=1)

    padded = -(-(steps + 1) // 16) * 16
    (
        arrived, block_out, alpha, inner, queries, keys, values, normalizer_out, max_out
    ) = exchange(
        (
            send_from,
            request_of,
            prompt_len[:, None, None],
            block_igate.astype(F32),
            block_fgate.astype(F32),
            stabilizer[:, :, None],
            normalizer,
            memory,
            block_q,
            block_k,
            block_v,
            step_igate.astype(F32),
            step_fgate.astype(F32),
            live.astype(jnp.int32)[:, None, None],
            step_q,
            step_k,
            step_v,
            out_weight,
        ),
        pair_cap,
        padded,
        2,
    )
    memory_out, step_hidden = decode_states(
        gather_from, arrived, queries, keys, values, alpha, inner, steps
    )
    step_out = project_sum(step_hidden, out_weight, "tensor", 1)[: slots * steps]
    return (
        block_out.reshape(requests, block, -1),
        step_out.reshape(slots, steps, -1),
        memory_out[:, None],
        normalizer_out,
        max_out[:, 0],
    )


def solution(mesh):
    rows = ("group", "pool")
    return jax.shard_map(
        body,
        mesh=mesh,
        in_specs=(
            P("group"),
            P(rows),
            P(rows, "tensor", None, None),
            P(rows, "tensor", None),
            P(rows, "tensor"),
            P(rows, None, "tensor"),
            P(rows, None, "tensor"),
            P(rows, None, "tensor"),
            P(rows, "tensor", None),
            P(rows, "tensor", None),
            P(rows, None, "tensor"),
            P(rows, None, "tensor"),
            P(rows, None, "tensor"),
            P(rows, "tensor", None),
            P(rows, "tensor", None),
            P("tensor", None),
        ),
        out_specs=(
            P(rows, None, "tensor"),
            P(rows, None, "tensor"),
            P(rows, "tensor", None, None),
            P(rows, "tensor", None),
            P(rows, "tensor"),
        ),
        check_vma=False,
    )
```

```python
import functools
import math

import jax
import jax.numpy as jnp
from jax import lax
from jax.experimental import pallas as pl
from jax.experimental.pallas import tpu as pltpu
from jax.sharding import PartitionSpec as P

F32 = jnp.float32
BF16 = jnp.bfloat16
MESH = pl.DeviceIdType.MESH
VMEM_LIMIT = 60 * 1024 * 1024


def gate_terms(igate, fgate, start):
    count = igate.shape[2]
    row = lax.broadcasted_iota(jnp.int32, (1, count, count), 1)
    column = lax.broadcasted_iota(jnp.int32, (1, count, count), 2)
    log_forget = jnp.minimum(fgate, 0.0) - jnp.log(1.0 + jnp.exp(-jnp.abs(fgate)))
    summed = jnp.sum(jnp.where(row >= column, log_forget, 0.0), axis=2, keepdims=True)
    across = jnp.sum(jnp.where(row == column, summed, 0.0), axis=1, keepdims=True)
    decays = jnp.where(row >= column, summed - across + igate, -jnp.inf)
    carried = summed + start
    running = jnp.maximum(carried, jnp.max(decays, axis=2, keepdims=True))
    weights = jnp.exp(decays - running)
    retained = jnp.exp(carried - running)
    return weights, retained, running


def lifted(ref):
    return ref[...].astype(F32)[:, None, :]


def as_column(rows):
    count = rows.shape[2]
    row = lax.broadcasted_iota(jnp.int32, (1, count, count), 1)
    column = lax.broadcasted_iota(jnp.int32, (1, count, count), 2)
    return jnp.sum(jnp.where(row == column, rows, 0.0), axis=2, keepdims=True)


def divisor(count, most):
    return max(d for d in range(1, most + 1) if count % d == 0)


def send_order(count):
    far = count // 2
    return sorted(range(1, count), key=lambda k: (abs(k - far), k))


def exchange_kernel(pool, heads, pair_cap, padded, *refs):
    (
        owner_map, prompt_len, stabilizer,
        igate, fgate, normalizer, memory, queries, keys, values,
        step_igate, step_fgate, step_q, step_k, step_v, weight,
        arrived, weight_out, gather_out, block_out, alpha_out, inner_out, query_out, key_out, value_out,
        normalizer_out, max_out,
        weights_s, retained_s, floor_s, used_s, keys_s, kept_s, small_s, begin_s, sent,
        hidden_s, weight_s, part_sent, part_held,
        small_send, small_recv, slot_send, slot_recv, part_send, part_recv,
        weight_send, weight_recv, own_sem, weight_sem, own_weight_sem,
    ) = refs
    axis_p, count_p = pool
    axis_t, count_t = heads
    me = lax.axis_index(axis_p)
    mine = lax.axis_index(axis_t)
    requests, block, dqk = keys.shape
    dv = values.shape[2]
    slots, steps = step_q.shape[:2]
    width = block_out.shape[1]
    scaling = 1.0 / math.sqrt(dqk)

    load_weight = pltpu.make_async_copy(weight, weight_s, weight_sem)
    load_weight.start()
    barrier = pltpu.get_barrier_semaphore()
    for k in range(1, count_p):
        pl.semaphore_signal(
            barrier, inc=1, device_id={axis_p: lax.rem(me + k, count_p)}, device_id_type=MESH
        )
    for k in range(1, count_t):
        pl.semaphore_signal(
            barrier, inc=1, device_id={axis_t: lax.rem(mine + k, count_t)}, device_id_type=MESH
        )

    request = lax.broadcasted_iota(jnp.int32, (requests, 1, 1), 0)
    length = jnp.zeros((requests, 1, 1), jnp.int32)
    start = jnp.zeros((requests, 1, 1), F32)
    for i in range(requests):
        length = jnp.where(request == i, prompt_len[i], length)
        start = jnp.where(request == i, stabilizer[i], start)
    weights, retained, running = gate_terms(lifted(igate), lifted(fgate), start)
    position = lax.broadcasted_iota(jnp.int32, (1, block, 1), 1)
    last = position == length - 1
    last_weights = jnp.sum(jnp.where(last, weights, 0.0), axis=1, keepdims=True)
    last_kept = jnp.sum(jnp.where(last, retained, 0.0), axis=1, keepdims=True)
    last_max = jnp.sum(jnp.where(last, running, 0.0), axis=1, keepdims=True)
    weighted_keys = keys[...].astype(F32) * as_column(last_weights)
    keys_s[...] = weighted_keys.astype(BF16)
    kept_s[...] = jnp.broadcast_to(last_kept, (requests, 1, dv))
    weights_s[...] = weights * scaling
    retained_s[...] = retained
    floor_s[...] = jnp.exp(-running)
    used_s[...] = jnp.where(position < length, 1.0, 0.0)
    own = pl.ds(me * requests, requests)
    small_s[own, :, :dqk] = last_kept * normalizer[...] + jnp.sum(
        weighted_keys, axis=1, keepdims=True
    )
    small_s[own, :, dqk:] = jnp.broadcast_to(last_max, (requests, 1, 128))

    pl.semaphore_wait(barrier, count_p + count_t - 2)
    small_copies = []
    for k in range(1, count_p):
        copy = pltpu.make_async_remote_copy(
            src_ref=small_s.at[own],
            dst_ref=small_s.at[own],
            send_sem=small_send.at[k - 1],
            recv_sem=small_recv.at[k - 1],
            device_id={axis_p: lax.rem(me + k, count_p)},
            device_id_type=MESH,
        )
        copy.start()
        small_copies.append(copy)

    owners = [owner_map[me * requests + r] for r in range(requests)]

    def taken_by(owner):
        found = jnp.int32(0)
        picked = [jnp.int32(0)] * pair_cap
        for r in range(requests):
            hit = owners[r] == owner
            picked = [
                jnp.where(hit & (found == j), r, index) for j, index in enumerate(picked)
            ]
            found = found + jnp.where(hit, 1, 0)
        return picked

    picks = [taken_by(lax.rem(me + k, count_p)) for k in range(count_p)]

    def pack(place, j):
        index = picks[place][j]
        outer = lax.dot_general(
            keys_s[index], values[index], (((0,), (0,)), ((), ())), preferred_element_type=F32
        )
        sent[place, j] = (memory[index].astype(F32) * kept_s[index] + outer).astype(BF16)

    slot_copies = []
    for j in range(pair_cap):
        for k in send_order(count_p):
            target = lax.rem(me + k, count_p)
            pack(k, j)
            copy = pltpu.make_async_remote_copy(
                src_ref=sent.at[k, j],
                dst_ref=arrived.at[me * pair_cap + j],
                send_sem=slot_send.at[k - 1, j],
                recv_sem=slot_recv.at[k - 1, j],
                device_id={axis_p: target},
                device_id_type=MESH,
            )
            copy.start()
            slot_copies.append(copy)
    for j in range(pair_cap):
        pack(0, j)
    keep_own = pltpu.make_async_copy(
        sent.at[0], arrived.at[pl.ds(me * pair_cap, pair_cap)], own_sem
    )
    keep_own.start()

    def columns_of(owner):
        return pl.ds(pl.multiple_of(owner * width, width), width)

    weight_copies = []
    for k in range(1, count_t):
        target = lax.rem(mine + k, count_t)
        copy = pltpu.make_async_remote_copy(
            src_ref=weight.at[:, columns_of(target)],
            dst_ref=weight_out.at[mine],
            send_sem=weight_send.at[k - 1],
            recv_sem=weight_recv.at[k - 1],
            device_id={axis_t: target},
            device_id_type=MESH,
        )
        copy.start()
        weight_copies.append(copy)
    own_weight = pltpu.make_async_copy(
        weight.at[:, columns_of(mine)], weight_out.at[mine], own_weight_sem
    )
    own_weight.start()

    @pl.loop(0, requests)
    def _(i):
        query, value = queries[i], values[i]
        scores = lax.dot_general(
            query, keys[i], (((1,), (1,)), ((), ())), preferred_element_type=F32
        )
        weighted = scores * weights_s[i]
        total = jnp.dot(weighted.astype(BF16), value, preferred_element_type=F32)
        recalled = jnp.dot(query, memory[i], preferred_element_type=F32)
        dots = jnp.sum(query.astype(F32) * normalizer[i], axis=1, keepdims=True)
        kept = retained_s[i] * scaling
        denominator = kept * dots + jnp.sum(weighted, axis=1, keepdims=True)
        denominator = jnp.maximum(jnp.abs(denominator), floor_s[i])
        result = (kept * recalled + total) / denominator
        result = jnp.where(used_s[i] > 0.0, result, 0.0)
        hidden_s[pl.ds(pl.multiple_of(i * block, block), block), :] = result.astype(BF16)

    load_weight.wait()

    def product(owner):
        return jnp.dot(
            hidden_s[...], weight_s[:, columns_of(owner)], preferred_element_type=F32
        ).astype(BF16)

    part_copies = []
    for k in range(1, count_t):
        target = lax.rem(mine + k, count_t)
        part_sent[k - 1] = product(target)
        copy = pltpu.make_async_remote_copy(
            src_ref=part_sent.at[k - 1],
            dst_ref=part_held.at[k - 1],
            send_sem=part_send.at[k - 1],
            recv_sem=part_recv.at[k - 1],
            device_id={axis_t: target},
            device_id_type=MESH,
        )
        copy.start()
        part_copies.append(copy)
    summed = product(mine).astype(F32)
    for k in range(1, count_t):
        part_copies[k - 1].wait_recv()
        summed = summed + part_held[k - 1].astype(F32)
    block_out[...] = summed.astype(BF16)

    for copy in small_copies:
        copy.wait_recv()

    def route(r, carry):
        rank, pair, request_of, landed = carry
        hit = owner_map[r] == me
        pair = jnp.where(lax.rem(r, requests) == 0, 0, pair)
        place = lax.div(r, requests) * pair_cap + pair
        here = [hit & (rank == s) for s in range(slots)]
        request_of = tuple(jnp.where(h, r, old) for h, old in zip(here, request_of))
        landed = tuple(jnp.where(h, place, old) for h, old in zip(here, landed))
        one = jnp.where(hit, 1, 0)
        return rank + one, pair + one, request_of, landed

    zero = jnp.int32(0)
    filled, _, request_of, landed = lax.fori_loop(
        0, count_p * requests, route, (zero, zero, (zero,) * slots, (zero,) * slots)
    )
    for s in range(slots):
        gather_out[s] = landed[s]
        begin_s[s] = small_s[request_of[s]]
    begin_normal = begin_s[:, :, :dqk]
    begin_max = begin_s[:, :, dqk : dqk + 1]
    alive = lax.broadcasted_iota(jnp.int32, (slots, 1, 1), 0) < filled
    weights, retained, running = gate_terms(
        lifted(step_igate), lifted(step_fgate), begin_max
    )
    query = step_q[...].astype(F32)
    key = step_k[...].astype(F32)
    value = step_v[...].astype(F32)
    dots = jnp.sum(query * begin_normal, axis=2, keepdims=True)
    denominator = retained * dots
    inner = jnp.zeros(value.shape, F32)
    for s in range(steps):
        scores = jnp.sum(query * key[:, s : s + 1, :], axis=2, keepdims=True)
        weighted = scores * weights[:, :, s : s + 1]
        denominator = denominator + weighted
        inner = inner + weighted * value[:, s : s + 1, :]
    denominator = jnp.maximum(jnp.abs(denominator * scaling), jnp.exp(-running))
    inner = jnp.where(alive, inner * scaling / denominator, 0.0)
    alpha = jnp.where(alive, retained * scaling / denominator, 0.0)
    last_row = slice(steps - 1, steps)
    step_keys = jnp.where(alive, key * as_column(weights[:, last_row, :]), 0.0)
    kept = jnp.where(alive, retained[:, last_row, :], 0.0)
    normalizer_out[...] = kept * begin_normal + jnp.sum(step_keys, axis=1, keepdims=True)
    max_out[...] = jnp.where(alive, running[:, last_row, :], 0.0)

    def pad(array):
        blank = jnp.zeros((slots, padded - steps, array.shape[2]), F32)
        return jnp.concatenate([array, blank], axis=1)

    query_out[...] = pad(query).astype(BF16)
    key_out[...] = pad(step_keys).astype(BF16)
    value_out[...] = pad(value).astype(BF16)
    inner_out[...] = pad(inner)
    blank = jnp.zeros((slots, padded - steps - 1, 1), F32)
    columns = jnp.concatenate([alpha, kept, blank], axis=1)
    alpha_out[...] = jnp.broadcast_to(columns, (slots, padded, 128))

    keep_own.wait()
    for copy in part_copies:
        copy.wait_send()
    for copy in small_copies:
        copy.wait_send()
    own_weight.wait()
    for copy in weight_copies:
        copy.wait()
    for copy in slot_copies:
        copy.wait()


def exchange(arrays, pair_cap, padded, collective_id):
    memory, values, step_q, weight = arrays[6], arrays[9], arrays[12], arrays[15]
    requests, dqk, dv = memory.shape
    block = values.shape[1]
    slots = step_q.shape[0]
    count_p, count_t = lax.axis_size("pool"), lax.axis_size("tensor")
    rows, width = requests * block, weight.shape[1] // count_t
    smem = pl.BlockSpec(memory_space=pltpu.SMEM)
    vmem = pl.BlockSpec(memory_space=pltpu.VMEM)
    anywhere = pl.BlockSpec(memory_space=pl.ANY)
    dma = pltpu.SemaphoreType.DMA
    shape = jax.ShapeDtypeStruct
    return pl.pallas_call(
        functools.partial(
            exchange_kernel, ("pool", count_p), ("tensor", count_t), pair_cap, padded
        ),
        out_shape=(
            shape((count_p * pair_cap, dqk, dv), BF16),
            shape((count_t, weight.shape[0], width), BF16),
            shape((slots,), jnp.int32),
            shape((rows, width), BF16),
            shape((slots, padded, 128), F32),
            shape((slots, padded, dv), F32),
            shape((slots, padded, dqk), BF16),
            shape((slots, padded, dqk), BF16),
            shape((slots, padded, dv), BF16),
            shape((slots, 1, dqk), F32),
            shape((slots, 1, 1), F32),
        ),
        in_specs=[smem] * 3 + [vmem] * 12 + [anywhere],
        out_specs=(anywhere, anywhere, smem) + (vmem,) * 8,
        scratch_shapes=[
            pltpu.VMEM((requests, block, block), F32),
            pltpu.VMEM((requests, block, 1), F32),
            pltpu.VMEM((requests, block, 1), F32),
            pltpu.VMEM((requests, block, 1), F32),
            pltpu.VMEM((requests, block, dqk), BF16),
            pltpu.VMEM((requests, 1, dv), F32),
            pltpu.VMEM((count_p * requests, 1, dqk + 128), F32),
            pltpu.VMEM((slots, 1, dqk + 128), F32),
            pltpu.VMEM((count_p, pair_cap, dqk, dv), BF16),
            pltpu.VMEM((rows, dv), BF16),
            pltpu.VMEM(weight.shape, BF16),
            pltpu.VMEM((count_t - 1, rows, width), BF16),
            pltpu.VMEM((count_t - 1, rows, width), BF16),
            dma((count_p - 1,)),
            dma((count_p - 1,)),
            dma((count_p - 1, pair_cap)),
            dma((count_p - 1, pair_cap)),
            dma((count_t - 1,)),
            dma((count_t - 1,)),
            dma((count_t - 1,)),
            dma((count_t - 1,)),
            dma,
            dma,
            dma,
        ],
        compiler_params=pltpu.CompilerParams(
            collective_id=collective_id, has_side_effects=True, vmem_limit_bytes=VMEM_LIMIT
        ),
    )(*arrays)


def decode_kernel(group, steps, pick, *refs):
    memories = refs[:group]
    queries, keys, values, alpha, inner, memory_out, hidden = refs[group:]
    step = pl.program_id(0)

    @pl.when(step == 0)
    def _():
        hidden[...] = jnp.zeros_like(hidden)

    rows = []
    for g in range(group):
        state = memories[g][0]
        recalled = jnp.dot(queries[g], state, preferred_element_type=F32)
        rows.append((alpha[g][:, :1] * recalled + inner[g])[:steps])
        outer = lax.dot_general(
            keys[g], values[g], (((0,), (0,)), ((), ())), preferred_element_type=F32
        )
        keep = alpha[g][steps : steps + 1, :1]
        memory_out[g] = (state.astype(F32) * keep + outer).astype(BF16)
    taken = group * steps
    hidden[pl.ds(pl.multiple_of(step * taken, taken), taken), :] = jnp.concatenate(rows, axis=0)


def decode_states(pick, arrived, queries, keys, values, alpha, inner, steps):
    slots, padded, dqk = queries.shape
    dv = values.shape[2]
    group = divisor(slots, 6)
    rows = -(-slots * steps // 16) * 16

    def spec(g):
        return pl.BlockSpec((1, dqk, dv), lambda i, pick: (pick[i * group + g], 0, 0))

    def part(width):
        return pl.BlockSpec((group, padded, width), lambda i, pick: (i, 0, 0))

    return pl.pallas_call(
        functools.partial(decode_kernel, group, steps),
        out_shape=(
            jax.ShapeDtypeStruct((slots, dqk, dv), BF16),
            jax.ShapeDtypeStruct((rows, dv), F32),
        ),
        grid_spec=pltpu.PrefetchScalarGridSpec(
            num_scalar_prefetch=1,
            grid=(slots // group,),
            in_specs=[spec(g) for g in range(group)]
            + [part(dqk), part(dqk), part(dv), part(128), part(dv)],
            out_specs=(
                pl.BlockSpec((group, dqk, dv), lambda i, pick: (i, 0, 0)),
                pl.BlockSpec((rows, dv), lambda i, pick: (0, 0)),
            ),
        ),
        compiler_params=pltpu.CompilerParams(vmem_limit_bytes=VMEM_LIMIT),
        cost_estimate=pl.CostEstimate(
            flops=4 * slots * padded * dqk * dv, bytes_accessed=4 * slots * dqk * dv, transcendentals=0
        ),
    )(pick, *([arrived] * group), queries, keys, values, alpha, inner)


def project_kernel(axis, count, hidden, weight, out, sent, held, send_sem, recv_sem):
    me = lax.axis_index(axis)
    barrier = pltpu.get_barrier_semaphore()
    for k in range(1, count):
        pl.semaphore_signal(
            barrier, inc=1, device_id={axis: lax.rem(me + k, count)}, device_id_type=MESH
        )
    sent[...] = hidden[...].astype(BF16)
    pl.semaphore_wait(barrier, count - 1)
    copies = []
    for k in range(1, count):
        copy = pltpu.make_async_remote_copy(
            src_ref=sent,
            dst_ref=held.at[k - 1],
            send_sem=send_sem.at[k - 1],
            recv_sem=recv_sem.at[k - 1],
            device_id={axis: lax.rem(me + k, count)},
            device_id_type=MESH,
        )
        copy.start()
        copies.append(copy)

    def product(rows, owner):
        terms = jnp.dot(rows, weight[owner], preferred_element_type=F32)
        return terms.astype(BF16).astype(F32)

    total = product(sent[...], me)
    for k in range(1, count):
        copies[k - 1].wait_recv()
        total = total + product(held[k - 1], lax.rem(me + count - k, count))
    out[...] = total.astype(BF16)
    for copy in copies:
        copy.wait_send()


def project_sum(hidden, weights, axis, collective_id):
    count, depth, width = weights.shape
    rows = hidden.shape[0]
    vmem = pl.BlockSpec(memory_space=pltpu.VMEM)
    return pl.pallas_call(
        functools.partial(project_kernel, axis, count),
        out_shape=jax.ShapeDtypeStruct((rows, width), BF16),
        in_specs=[vmem, vmem],
        out_specs=vmem,
        scratch_shapes=[
            pltpu.VMEM((rows, depth), BF16),
            pltpu.VMEM((count - 1, rows, depth), BF16),
            pltpu.SemaphoreType.DMA((count - 1,)),
            pltpu.SemaphoreType.DMA((count - 1,)),
        ],
        compiler_params=pltpu.CompilerParams(
            collective_id=collective_id, has_side_effects=True, vmem_limit_bytes=VMEM_LIMIT
        ),
        cost_estimate=pl.CostEstimate(
            flops=2 * rows * weights.size,
            bytes_accessed=2 * weights.size,
            transcendentals=0,
        ),
    )(hidden, weights)


def body(
    owner_map,
    prompt_len,
    memory,
    normalizer,
    stabilizer,
    block_q,
    block_k,
    block_v,
    block_igate,
    block_fgate,
    step_q,
    step_k,
    step_v,
    step_igate,
    step_fgate,
    out_weight,
):
    pool_size = lax.axis_size("pool")
    requests, block = block_q.shape[:2]
    dqk, dv = memory.shape[2:]
    slots, steps = step_q.shape[:2]
    capacity = requests + requests // 2
    pair_cap = (capacity + pool_size - 1) // pool_size
    memory = memory.reshape(requests, dqk, dv)

    padded = -(-(steps + 1) // 16) * 16
    (
        arrived, weights, gather_from, block_out, alpha, inner, queries, keys, values, normalizer_out, max_out
    ) = exchange(
        (
            owner_map,
            prompt_len,
            stabilizer[:, 0],
            block_igate[:, 0],
            block_fgate[:, 0],
            normalizer,
            memory,
            block_q,
            block_k,
            block_v,
            step_igate[:, 0],
            step_fgate[:, 0],
            step_q,
            step_k,
            step_v,
            out_weight,
        ),
        pair_cap,
        padded,
        2,
    )
    memory_out, step_hidden = decode_states(
        gather_from, arrived, queries, keys, values, alpha, inner, steps
    )
    step_out = project_sum(step_hidden, weights, "tensor", 1)[: slots * steps]
    return (
        block_out.reshape(requests, block, -1),
        step_out.reshape(slots, steps, -1),
        memory_out[:, None],
        normalizer_out,
        max_out[:, 0],
    )


def solution(mesh):
    rows = ("group", "pool")
    return jax.shard_map(
        body,
        mesh=mesh,
        in_specs=(
            P("group"),
            P(rows),
            P(rows, "tensor", None, None),
            P(rows, "tensor", None),
            P(rows, "tensor"),
            P(rows, None, "tensor"),
            P(rows, None, "tensor"),
            P(rows, None, "tensor"),
            P(rows, "tensor", None),
            P(rows, "tensor", None),
            P(rows, None, "tensor"),
            P(rows, None, "tensor"),
            P(rows, None, "tensor"),
            P(rows, "tensor", None),
            P(rows, "tensor", None),
            P("tensor", None),
        ),
        out_specs=(
            P(rows, None, "tensor"),
            P(rows, None, "tensor"),
            P(rows, "tensor", None, None),
            P(rows, "tensor", None),
            P(rows, "tensor"),
        ),
        check_vma=False,
    )
```

```python
import functools
import math

import jax
import jax.numpy as jnp
from jax import lax
from jax.experimental import pallas as pl
from jax.experimental.pallas import tpu as pltpu
from jax.sharding import PartitionSpec as P

F32 = jnp.float32
BF16 = jnp.bfloat16
MESH = pl.DeviceIdType.MESH
VMEM_LIMIT = 60 * 1024 * 1024


def gate_terms(igate, fgate, start):
    count = igate.shape[2]
    row = lax.broadcasted_iota(jnp.int32, (1, count, count), 1)
    column = lax.broadcasted_iota(jnp.int32, (1, count, count), 2)
    log_forget = jnp.minimum(fgate, 0.0) - jnp.log(1.0 + jnp.exp(-jnp.abs(fgate)))
    summed = jnp.sum(jnp.where(row >= column, log_forget, 0.0), axis=2, keepdims=True)
    across = jnp.sum(jnp.where(row == column, summed, 0.0), axis=1, keepdims=True)
    decays = jnp.where(row >= column, summed - across + igate, -jnp.inf)
    carried = summed + start
    running = jnp.maximum(carried, jnp.max(decays, axis=2, keepdims=True))
    weights = jnp.exp(decays - running)
    retained = jnp.exp(carried - running)
    return weights, retained, running


def lifted(ref, turned=False):
    rows = ref[...].astype(F32)
    return (rows.T if turned else rows)[:, None, :]


def as_column(rows):
    count = rows.shape[2]
    row = lax.broadcasted_iota(jnp.int32, (1, count, count), 1)
    column = lax.broadcasted_iota(jnp.int32, (1, count, count), 2)
    return jnp.sum(jnp.where(row == column, rows, 0.0), axis=2, keepdims=True)


def divisor(count, most):
    return max(d for d in range(1, most + 1) if count % d == 0)


def send_order(count):
    far = count // 2
    return sorted(range(1, count), key=lambda k: (abs(k - far), k))


def exchange_kernel(pool, heads, pair_cap, padded, *refs):
    (
        owner_map, prompt_len, stabilizer,
        igate, fgate, normalizer, memory, queries, keys, values,
        step_igate, step_fgate, step_q, step_k, step_v, weight,
        arrived, weight_out, gather_out, block_out, alpha_out, inner_out, query_out, key_out, value_out,
        normalizer_out, max_out,
        weights_s, retained_s, floor_s, used_s, keys_s, kept_s, small_s, begin_s, sent,
        hidden_s, weight_s, part_sent, part_held,
        small_send, small_recv, slot_send, slot_recv, part_send, part_recv,
        weight_send, weight_recv, own_sem, weight_sem, own_weight_sem,
    ) = refs
    axis_p, count_p = pool
    axis_t, count_t = heads
    me = lax.axis_index(axis_p)
    mine = lax.axis_index(axis_t)
    requests, block, dqk = keys.shape
    dv = values.shape[2]
    slots, steps = step_q.shape[:2]
    width = block_out.shape[1]
    scaling = 1.0 / math.sqrt(dqk)

    load_weight = pltpu.make_async_copy(weight, weight_s, weight_sem)
    load_weight.start()
    barrier = pltpu.get_barrier_semaphore()
    for k in range(1, count_p):
        pl.semaphore_signal(
            barrier, inc=1, device_id={axis_p: lax.rem(me + k, count_p)}, device_id_type=MESH
        )
    for k in range(1, count_t):
        pl.semaphore_signal(
            barrier, inc=1, device_id={axis_t: lax.rem(mine + k, count_t)}, device_id_type=MESH
        )

    request = lax.broadcasted_iota(jnp.int32, (requests, 1, 1), 0)
    length = jnp.zeros((requests, 1, 1), jnp.int32)
    start = jnp.zeros((requests, 1, 1), F32)
    for i in range(requests):
        length = jnp.where(request == i, prompt_len[i], length)
        start = jnp.where(request == i, stabilizer[i], start)
    weights, retained, running = gate_terms(lifted(igate), lifted(fgate), start)
    position = lax.broadcasted_iota(jnp.int32, (1, block, 1), 1)
    last = position == length - 1
    last_weights = jnp.sum(jnp.where(last, weights, 0.0), axis=1, keepdims=True)
    last_kept = jnp.sum(jnp.where(last, retained, 0.0), axis=1, keepdims=True)
    last_max = jnp.sum(jnp.where(last, running, 0.0), axis=1, keepdims=True)
    weighted_keys = keys[...].astype(F32) * as_column(last_weights)
    keys_s[...] = weighted_keys.astype(BF16)
    kept_s[...] = jnp.broadcast_to(last_kept, (requests, 1, dv))
    weights_s[...] = weights * scaling
    retained_s[...] = retained
    floor_s[...] = jnp.exp(-running)
    used_s[...] = jnp.where(position < length, 1.0, 0.0)
    own = pl.ds(me * requests, requests)
    small_s[own, :, :dqk] = last_kept * normalizer[...] + jnp.sum(
        weighted_keys, axis=1, keepdims=True
    )
    small_s[own, :, dqk:] = jnp.broadcast_to(last_max, (requests, 1, 128))

    pl.semaphore_wait(barrier, count_p + count_t - 2)
    small_copies = []
    for k in range(1, count_p):
        copy = pltpu.make_async_remote_copy(
            src_ref=small_s.at[own],
            dst_ref=small_s.at[own],
            send_sem=small_send.at[k - 1],
            recv_sem=small_recv.at[k - 1],
            device_id={axis_p: lax.rem(me + k, count_p)},
            device_id_type=MESH,
        )
        copy.start()
        small_copies.append(copy)

    owners = [owner_map[me * requests + r] for r in range(requests)]

    def taken_by(owner):
        found = jnp.int32(0)
        picked = [jnp.int32(0)] * pair_cap
        for r in range(requests):
            hit = owners[r] == owner
            picked = [
                jnp.where(hit & (found == j), r, index) for j, index in enumerate(picked)
            ]
            found = found + jnp.where(hit, 1, 0)
        return picked

    picks = [taken_by(lax.rem(me + k, count_p)) for k in range(count_p)]

    def pack(place, j):
        index = picks[place][j]
        outer = lax.dot_general(
            keys_s[index], values[index], (((0,), (0,)), ((), ())), preferred_element_type=F32
        )
        sent[place, j] = (memory[index].astype(F32) * kept_s[index] + outer).astype(BF16)

    slot_copies = []
    for j in range(pair_cap):
        for k in send_order(count_p):
            target = lax.rem(me + k, count_p)
            pack(k, j)
            copy = pltpu.make_async_remote_copy(
                src_ref=sent.at[k, j],
                dst_ref=arrived.at[me * pair_cap + j],
                send_sem=slot_send.at[k - 1, j],
                recv_sem=slot_recv.at[k - 1, j],
                device_id={axis_p: target},
                device_id_type=MESH,
            )
            copy.start()
            slot_copies.append(copy)
    for j in range(pair_cap):
        pack(0, j)
    keep_own = pltpu.make_async_copy(
        sent.at[0], arrived.at[pl.ds(me * pair_cap, pair_cap)], own_sem
    )
    keep_own.start()

    def columns_of(owner):
        return pl.ds(pl.multiple_of(owner * width, width), width)

    weight_copies = []
    for k in range(1, count_t):
        target = lax.rem(mine + k, count_t)
        copy = pltpu.make_async_remote_copy(
            src_ref=weight.at[:, columns_of(target)],
            dst_ref=weight_out.at[mine],
            send_sem=weight_send.at[k - 1],
            recv_sem=weight_recv.at[k - 1],
            device_id={axis_t: target},
            device_id_type=MESH,
        )
        copy.start()
        weight_copies.append(copy)
    own_weight = pltpu.make_async_copy(
        weight.at[:, columns_of(mine)], weight_out.at[mine], own_weight_sem
    )
    own_weight.start()

    @pl.loop(0, requests)
    def _(i):
        query, value = queries[i], values[i]
        scores = lax.dot_general(
            query, keys[i], (((1,), (1,)), ((), ())), preferred_element_type=F32
        )
        weighted = scores * weights_s[i]
        total = jnp.dot(weighted.astype(BF16), value, preferred_element_type=F32)
        recalled = jnp.dot(query, memory[i], preferred_element_type=F32)
        dots = jnp.sum(query.astype(F32) * normalizer[i], axis=1, keepdims=True)
        kept = retained_s[i] * scaling
        denominator = kept * dots + jnp.sum(weighted, axis=1, keepdims=True)
        denominator = jnp.maximum(jnp.abs(denominator), floor_s[i])
        result = (kept * recalled + total) / denominator
        result = jnp.where(used_s[i] > 0.0, result, 0.0)
        hidden_s[pl.ds(pl.multiple_of(i * block, block), block), :] = result.astype(BF16)

    load_weight.wait()

    def product(owner):
        return jnp.dot(
            hidden_s[...], weight_s[:, columns_of(owner)], preferred_element_type=F32
        ).astype(BF16)

    part_copies = []
    for k in range(1, count_t):
        target = lax.rem(mine + k, count_t)
        part_sent[k - 1] = product(target)
        copy = pltpu.make_async_remote_copy(
            src_ref=part_sent.at[k - 1],
            dst_ref=part_held.at[k - 1],
            send_sem=part_send.at[k - 1],
            recv_sem=part_recv.at[k - 1],
            device_id={axis_t: target},
            device_id_type=MESH,
        )
        copy.start()
        part_copies.append(copy)
    summed = product(mine).astype(F32)
    for k in range(1, count_t):
        part_copies[k - 1].wait_recv()
        summed = summed + part_held[k - 1].astype(F32)
    block_out[...] = summed.astype(BF16)

    for copy in small_copies:
        copy.wait_recv()

    def route(r, carry):
        rank, pair, request_of, landed = carry
        hit = owner_map[r] == me
        pair = jnp.where(lax.rem(r, requests) == 0, 0, pair)
        place = lax.div(r, requests) * pair_cap + pair
        here = [hit & (rank == s) for s in range(slots)]
        request_of = tuple(jnp.where(h, r, old) for h, old in zip(here, request_of))
        landed = tuple(jnp.where(h, place, old) for h, old in zip(here, landed))
        one = jnp.where(hit, 1, 0)
        return rank + one, pair + one, request_of, landed

    zero = jnp.int32(0)
    filled, _, request_of, landed = lax.fori_loop(
        0, count_p * requests, route, (zero, zero, (zero,) * slots, (zero,) * slots)
    )
    for s in range(slots):
        gather_out[s] = landed[s]
        begin_s[s] = small_s[request_of[s]]
    begin_normal = begin_s[:, :, :dqk]
    begin_max = begin_s[:, :, dqk : dqk + 1]
    alive = lax.broadcasted_iota(jnp.int32, (slots, 1, 1), 0) < filled
    weights, retained, running = gate_terms(
        lifted(step_igate, True), lifted(step_fgate, True), begin_max
    )
    query = step_q[...].astype(F32)
    key = step_k[...].astype(F32)
    value = step_v[...].astype(F32)
    dots = jnp.sum(query * begin_normal, axis=2, keepdims=True)
    denominator = retained * dots
    inner = jnp.zeros(value.shape, F32)
    for s in range(steps):
        scores = jnp.sum(query * key[:, s : s + 1, :], axis=2, keepdims=True)
        weighted = scores * weights[:, :, s : s + 1]
        denominator = denominator + weighted
        inner = inner + weighted * value[:, s : s + 1, :]
    denominator = jnp.maximum(jnp.abs(denominator * scaling), jnp.exp(-running))
    inner = jnp.where(alive, inner * scaling / denominator, 0.0)
    alpha = jnp.where(alive, retained * scaling / denominator, 0.0)
    last_row = slice(steps - 1, steps)
    step_keys = jnp.where(alive, key * as_column(weights[:, last_row, :]), 0.0)
    kept = jnp.where(alive, retained[:, last_row, :], 0.0)
    normalizer_out[...] = kept * begin_normal + jnp.sum(step_keys, axis=1, keepdims=True)
    finals = jnp.where(alive, running[:, last_row, :], 0.0)
    lane = lax.broadcasted_iota(jnp.int32, (1, slots), 1)
    row = jnp.zeros((1, slots), F32)
    for s in range(slots):
        row = jnp.where(lane == s, finals[s], row)
    max_out[...] = row

    def pad(array):
        blank = jnp.zeros((slots, padded - steps, array.shape[2]), F32)
        return jnp.concatenate([array, blank], axis=1)

    query_out[...] = pad(query).astype(BF16)
    key_out[...] = pad(step_keys).astype(BF16)
    value_out[...] = pad(value).astype(BF16)
    inner_out[...] = pad(inner)
    blank = jnp.zeros((slots, padded - steps - 1, 1), F32)
    columns = jnp.concatenate([alpha, kept, blank], axis=1)
    alpha_out[...] = jnp.broadcast_to(columns, (slots, padded, 128))

    keep_own.wait()
    for copy in part_copies:
        copy.wait_send()
    for copy in small_copies:
        copy.wait_send()
    own_weight.wait()
    for copy in weight_copies:
        copy.wait()
    for copy in slot_copies:
        copy.wait()


def exchange(arrays, pair_cap, padded, collective_id):
    memory, values, step_q, weight = arrays[6], arrays[9], arrays[12], arrays[15]
    requests, dqk, dv = memory.shape
    block = values.shape[1]
    slots = step_q.shape[0]
    count_p, count_t = lax.axis_size("pool"), lax.axis_size("tensor")
    rows, width = requests * block, weight.shape[1] // count_t
    smem = pl.BlockSpec(memory_space=pltpu.SMEM)
    vmem = pl.BlockSpec(memory_space=pltpu.VMEM)
    anywhere = pl.BlockSpec(memory_space=pl.ANY)
    dma = pltpu.SemaphoreType.DMA
    shape = jax.ShapeDtypeStruct
    return pl.pallas_call(
        functools.partial(
            exchange_kernel, ("pool", count_p), ("tensor", count_t), pair_cap, padded
        ),
        out_shape=(
            shape((count_p * pair_cap, dqk, dv), BF16),
            shape((count_t, weight.shape[0], width), BF16),
            shape((slots,), jnp.int32),
            shape((rows, width), BF16),
            shape((slots, padded, 128), F32),
            shape((slots, padded, dv), F32),
            shape((slots, padded, dqk), BF16),
            shape((slots, padded, dqk), BF16),
            shape((slots, padded, dv), BF16),
            shape((slots, 1, dqk), F32),
            shape((1, slots), F32),
        ),
        in_specs=[smem] * 3 + [vmem] * 12 + [anywhere],
        out_specs=(anywhere, anywhere, smem) + (vmem,) * 8,
        scratch_shapes=[
            pltpu.VMEM((requests, block, block), F32),
            pltpu.VMEM((requests, block, 1), F32),
            pltpu.VMEM((requests, block, 1), F32),
            pltpu.VMEM((requests, block, 1), F32),
            pltpu.VMEM((requests, block, dqk), BF16),
            pltpu.VMEM((requests, 1, dv), F32),
            pltpu.VMEM((count_p * requests, 1, dqk + 128), F32),
            pltpu.VMEM((slots, 1, dqk + 128), F32),
            pltpu.VMEM((count_p, pair_cap, dqk, dv), BF16),
            pltpu.VMEM((rows, dv), BF16),
            pltpu.VMEM(weight.shape, BF16),
            pltpu.VMEM((count_t - 1, rows, width), BF16),
            pltpu.VMEM((count_t - 1, rows, width), BF16),
            dma((count_p - 1,)),
            dma((count_p - 1,)),
            dma((count_p - 1, pair_cap)),
            dma((count_p - 1, pair_cap)),
            dma((count_t - 1,)),
            dma((count_t - 1,)),
            dma((count_t - 1,)),
            dma((count_t - 1,)),
            dma,
            dma,
            dma,
        ],
        compiler_params=pltpu.CompilerParams(
            collective_id=collective_id, has_side_effects=True, vmem_limit_bytes=VMEM_LIMIT
        ),
    )(*arrays)


def decode_kernel(group, steps, pick, *refs):
    memories = refs[:group]
    queries, keys, values, alpha, inner, memory_out, hidden = refs[group:]
    step = pl.program_id(0)

    @pl.when(step == 0)
    def _():
        hidden[...] = jnp.zeros_like(hidden)

    rows = []
    for g in range(group):
        state = memories[g][0]
        recalled = jnp.dot(queries[g], state, preferred_element_type=F32)
        rows.append((alpha[g][:, :1] * recalled + inner[g])[:steps])
        outer = lax.dot_general(
            keys[g], values[g], (((0,), (0,)), ((), ())), preferred_element_type=F32
        )
        keep = alpha[g][steps : steps + 1, :1]
        memory_out[g] = (state.astype(F32) * keep + outer).astype(BF16)
    taken = group * steps
    hidden[pl.ds(pl.multiple_of(step * taken, taken), taken), :] = jnp.concatenate(rows, axis=0)


def decode_states(pick, arrived, queries, keys, values, alpha, inner, steps):
    slots, padded, dqk = queries.shape
    dv = values.shape[2]
    group = divisor(slots, 6)
    rows = -(-slots * steps // 16) * 16

    def spec(g):
        return pl.BlockSpec((1, dqk, dv), lambda i, pick: (pick[i * group + g], 0, 0))

    def part(width):
        return pl.BlockSpec((group, padded, width), lambda i, pick: (i, 0, 0))

    return pl.pallas_call(
        functools.partial(decode_kernel, group, steps),
        out_shape=(
            jax.ShapeDtypeStruct((slots, dqk, dv), BF16),
            jax.ShapeDtypeStruct((rows, dv), F32),
        ),
        grid_spec=pltpu.PrefetchScalarGridSpec(
            num_scalar_prefetch=1,
            grid=(slots // group,),
            in_specs=[spec(g) for g in range(group)]
            + [part(dqk), part(dqk), part(dv), part(128), part(dv)],
            out_specs=(
                pl.BlockSpec((group, dqk, dv), lambda i, pick: (i, 0, 0)),
                pl.BlockSpec((rows, dv), lambda i, pick: (0, 0)),
            ),
        ),
        compiler_params=pltpu.CompilerParams(vmem_limit_bytes=VMEM_LIMIT),
        cost_estimate=pl.CostEstimate(
            flops=4 * slots * padded * dqk * dv, bytes_accessed=4 * slots * dqk * dv, transcendentals=0
        ),
    )(pick, *([arrived] * group), queries, keys, values, alpha, inner)


def project_kernel(
    axis, count, hidden, weight_in, out, weight, sent, held, send_sem, recv_sem, weight_sem
):
    me = lax.axis_index(axis)
    load_weight = pltpu.make_async_copy(weight_in, weight, weight_sem)
    load_weight.start()
    barrier = pltpu.get_barrier_semaphore()
    for k in range(1, count):
        pl.semaphore_signal(
            barrier, inc=1, device_id={axis: lax.rem(me + k, count)}, device_id_type=MESH
        )
    sent[...] = hidden[...].astype(BF16)
    pl.semaphore_wait(barrier, count - 1)
    copies = []
    for k in range(1, count):
        copy = pltpu.make_async_remote_copy(
            src_ref=sent,
            dst_ref=held.at[k - 1],
            send_sem=send_sem.at[k - 1],
            recv_sem=recv_sem.at[k - 1],
            device_id={axis: lax.rem(me + k, count)},
            device_id_type=MESH,
        )
        copy.start()
        copies.append(copy)

    def product(rows, owner):
        terms = jnp.dot(rows, weight[owner], preferred_element_type=F32)
        return terms.astype(BF16).astype(F32)

    load_weight.wait()
    total = product(sent[...], me)
    for k in range(1, count):
        copies[k - 1].wait_recv()
        total = total + product(held[k - 1], lax.rem(me + count - k, count))
    slots, steps = out.shape[:2]
    for s in range(slots):
        out[s] = total[s * steps : (s + 1) * steps].astype(BF16)
    for copy in copies:
        copy.wait_send()


def project_sum(hidden, weights, slots, steps, axis, collective_id):
    count, depth, width = weights.shape
    rows = hidden.shape[0]
    vmem = pl.BlockSpec(memory_space=pltpu.VMEM)
    return pl.pallas_call(
        functools.partial(project_kernel, axis, count),
        out_shape=jax.ShapeDtypeStruct((slots, steps, width), BF16),
        in_specs=[vmem, pl.BlockSpec(memory_space=pl.ANY)],
        out_specs=vmem,
        scratch_shapes=[
            pltpu.VMEM(weights.shape, BF16),
            pltpu.VMEM((rows, depth), BF16),
            pltpu.VMEM((count - 1, rows, depth), BF16),
            pltpu.SemaphoreType.DMA((count - 1,)),
            pltpu.SemaphoreType.DMA((count - 1,)),
            pltpu.SemaphoreType.DMA,
        ],
        compiler_params=pltpu.CompilerParams(
            collective_id=collective_id, has_side_effects=True, vmem_limit_bytes=VMEM_LIMIT
        ),
        cost_estimate=pl.CostEstimate(
            flops=2 * rows * weights.size,
            bytes_accessed=2 * weights.size,
            transcendentals=0,
        ),
    )(hidden, weights)


def body(
    owner_map,
    prompt_len,
    memory,
    normalizer,
    stabilizer,
    block_q,
    block_k,
    block_v,
    block_igate,
    block_fgate,
    step_q,
    step_k,
    step_v,
    step_igate,
    step_fgate,
    out_weight,
):
    pool_size = lax.axis_size("pool")
    requests, block = block_q.shape[:2]
    dqk, dv = memory.shape[2:]
    slots, steps = step_q.shape[:2]
    capacity = requests + requests // 2
    pair_cap = (capacity + pool_size - 1) // pool_size
    memory = memory.reshape(requests, dqk, dv)

    padded = -(-(steps + 1) // 16) * 16
    (
        arrived, weights, gather_from, block_out, alpha, inner, queries, keys, values, normalizer_out, max_out
    ) = exchange(
        (
            owner_map,
            prompt_len,
            stabilizer[:, 0],
            block_igate[:, 0],
            block_fgate[:, 0],
            normalizer,
            memory,
            block_q,
            block_k,
            block_v,
            step_igate[:, 0].T,
            step_fgate[:, 0].T,
            step_q,
            step_k,
            step_v,
            out_weight,
        ),
        pair_cap,
        padded,
        2,
    )
    memory_out, step_hidden = decode_states(
        gather_from, arrived, queries, keys, values, alpha, inner, steps
    )
    step_out = project_sum(step_hidden, weights, slots, steps, "tensor", 1)
    return (
        block_out.reshape(requests, block, -1),
        step_out,
        memory_out[:, None],
        normalizer_out,
        max_out.reshape(slots, 1),
    )


def solution(mesh):
    rows = ("group", "pool")
    return jax.shard_map(
        body,
        mesh=mesh,
        in_specs=(
            P("group"),
            P(rows),
            P(rows, "tensor", None, None),
            P(rows, "tensor", None),
            P(rows, "tensor"),
            P(rows, None, "tensor"),
            P(rows, None, "tensor"),
            P(rows, None, "tensor"),
            P(rows, "tensor", None),
            P(rows, "tensor", None),
            P(rows, None, "tensor"),
            P(rows, None, "tensor"),
            P(rows, None, "tensor"),
            P(rows, "tensor", None),
            P(rows, "tensor", None),
            P("tensor", None),
        ),
        out_specs=(
            P(rows, None, "tensor"),
            P(rows, None, "tensor"),
            P(rows, "tensor", None, None),
            P(rows, "tensor", None),
            P(rows, "tensor"),
        ),
        check_vma=False,
    )
```
